32 devices in a mesh: space: 8 (over z, x), bins: 4 (over y, core).
Axes of the slice: x: 2, y: 2, z: 4, core: 2. Of those that a mesh axis runs over, the one named last changes fastest.
Arguments:
- spectrum: bfloat16 [1152, 192, 64], P('bins', 'space'), may hold values from 0.099609375 to 2
- group_speed: float32 [2, 1152], P(None, 'bins'), may hold values from -0.3 to 0.3
- stokes_kernel: bfloat16 [1152, 128], P('bins'), may hold values from -0.1875 to 0.1875
- pair_bins: int32 [3, 4608], replicated, may hold values from 0 to 1151
- pair_coef: float32 [4608], replicated, may hold values from -3 to 3
- currents: float32 [64, 192, 128], P(('space', 'bins')), may hold values from -6 to 6
- col_map: int32 [32], replicated, may hold values from 0 to 31, each once
- wave_wet: int32 [192, 64], P('space'), may hold values 0 or 1
- ocean_wet: int32 [64, 192], P(('space', 'bins')), may hold values 0 or 1
Outputs:
- new_spectrum: bfloat16 [1152, 192, 64], P(None, ('space', 'bins'))
- new_currents: float32 [64, 192, 128], P(('space', 'bins'))
The draws below stay inside these ranges and needn't reach their ends.
All inputs are finite; a program needn't handle non-finite values. No bound on the sum of `wave_wet` or of `ocean_wet` on one device may be relied on, other than what follows from the above.
Results may differ from the reference program's by a relative error of at most 0.0052.
Values may be sent and summed in bfloat16 or wider, within the bound.
A program may use at most 64 MiB of HBM per device.

```python
import math
import jax
import jax.numpy as jnp
from jax import lax

NBINS = 1152
LEV = 64
NPAIRS = 4608
OCOLS = 2
NX = 192
GY = 64
OGROUPS = 32


def plant(array, stream_key, low, largest):
    index_at = [jax.random.randint(jax.random.fold_in(stream_key, axis), (), 0, length) for axis, length in enumerate(array.shape)]
    main_axis = array.shape.index(max(array.shape))
    neighbour = index_at[:main_axis] + [(index_at[main_axis] + 1) % array.shape[main_axis]] + index_at[main_axis + 1:]
    return array.at[tuple(index_at)].set(low).at[tuple(neighbour)].set(largest)


def levels(rng, extent, cuts, least, high):
    factor_of = 1.0
    for dim, shards_of in cuts:
        steps = jax.random.uniform(jax.random.fold_in(jax.random.fold_in(rng, 6), dim), (shards_of,), jnp.float32, least / len(cuts), high / len(cuts))
        factor_of = factor_of * jnp.repeat(jnp.exp(steps), extent[dim] // shards_of).reshape((-1,) + (1,) * (len(extent) - 1 - dim))
    return factor_of


def noise(rng, extent, width, bound, cuts=(), kind=jnp.bfloat16):
    gain = levels(rng, extent, cuts, -0.22, 0.18) if cuts else 1.0
    values = jax.random.normal(rng, extent, jnp.float32) * width * gain
    return jnp.minimum(jnp.maximum(values, -bound), bound).astype(kind)


def setup_inputs(seed: int = 0) -> dict:
    key_list = jax.random.split(jax.random.key(seed), 10)
    return {
        "spectrum": jnp.clip(jnp.exp(math.log(2.0) - 2.9996462 * jax.random.uniform(key_list[0], (NBINS, NX, GY), jnp.float32) ** levels(key_list[0], (NBINS, NX, GY), ((0, 4), (1, 8)), -0.2, 0.2)), 0.099609375, 2.0).astype(jnp.bfloat16),
        "group_speed": jnp.clip(jax.random.uniform(key_list[1], (2, NBINS), jnp.float32, -0.3, 0.3) * levels(key_list[1], (2, NBINS), ((1, 4),), -0.4, 0.0), -0.3, 0.3),
        "stokes_kernel": noise(key_list[2], (NBINS, 2 * LEV), NBINS ** -0.5, 0.1875, ((0, 4),)),
        "pair_bins": plant(jax.random.randint(key_list[3], (3, NPAIRS), 0, NBINS), jax.random.fold_in(key_list[3], 1), 0, NBINS - 1).astype(jnp.int32),
        "pair_coef": noise(key_list[4], (NPAIRS,), 0.5, 3.0, (), jnp.float32),
        "currents": noise(key_list[5], (GY, NX, 2 * LEV), 1.0, 6.0, ((0, 32),), jnp.float32),
        "col_map": jax.random.permutation(key_list[6], OGROUPS).astype(jnp.int32),
        "wave_wet": plant((jax.random.randint(key_list[7], (NX, GY), 0, 5) < 4).astype(jnp.int32), jax.random.fold_in(key_list[7], 1), 0, 1),
        "ocean_wet": plant((jax.random.randint(key_list[8], (GY, NX), 0, 5) < 4).astype(jnp.int32), jax.random.fold_in(key_list[8], 1), 0, 1),
    }


DT_OCEAN = 0.5
CORIOLIS = 0.8
MIXING = 0.4
CURRENT_SCALE = 0.15
DT_SOURCE = 0.5


def levels_laplacian(field):
    upper = jnp.concatenate([field[..., :1], field[..., :-1]], axis=-1)
    lower = jnp.concatenate([field[..., 1:], field[..., -1:]], axis=-1)
    return upper + lower - 2.0 * field


def ocean_step(currents, drift, wet):
    east = currents[..., :LEV]
    north = currents[..., LEV:]
    east_drift = drift[..., :LEV]
    north_drift = drift[..., LEV:]
    new_east = east + DT_OCEAN * (CORIOLIS * (north + north_drift) + MIXING * levels_laplacian(east))
    new_north = north + DT_OCEAN * (-CORIOLIS * (east + east_drift) + MIXING * levels_laplacian(north))
    return wet[..., None].astype(jnp.float32) * jnp.concatenate([new_east, new_north], axis=-1)


def advect_bin(energy, speed_x, speed_y, cur, wet):
    energy = energy.astype(jnp.float32)
    cx = speed_x + cur[0]
    cy = speed_y + cur[1]
    plus_x = jnp.maximum(cx, 0.0) * energy
    minus_x = jnp.minimum(cx, 0.0) * energy
    plus_y = jnp.maximum(cy, 0.0) * energy
    minus_y = jnp.minimum(cy, 0.0) * energy
    plus_x_prev = jnp.pad(plus_x[:-1, :], ((1, 0), (0, 0)))
    minus_x_next = jnp.pad(minus_x[1:, :], ((0, 1), (0, 0)))
    plus_y_prev = jnp.pad(plus_y[:, :-1], ((0, 0), (1, 0)))
    minus_y_next = jnp.pad(minus_y[:, 1:], ((0, 0), (0, 1)))
    result = energy - plus_x + plus_x_prev - minus_x_next + minus_x - plus_y + plus_y_prev - minus_y_next + minus_y
    return (wet.astype(jnp.float32) * result).astype(jnp.bfloat16)


def reference(spectrum, group_speed, stokes_kernel, pair_bins, pair_coef, currents, col_map, wave_wet, ocean_wet):
    slot_col = (col_map[:, None] * OCOLS + jnp.arange(OCOLS, dtype=jnp.int32)[None, :]).reshape(-1).astype(jnp.int32)
    drift_cols = jnp.einsum('kxc,kl->cxl', spectrum.astype(jnp.float32), stokes_kernel.astype(jnp.float32))
    drift = jnp.take(drift_cols, slot_col, axis=0)
    new_currents = ocean_step(currents, drift, ocean_wet)
    surface = jnp.stack([new_currents[:, :, 0], new_currents[:, :, LEV]])
    inverse = jnp.argsort(slot_col).astype(jnp.int32)
    cur = CURRENT_SCALE * jnp.tanh(jnp.transpose(jnp.take(surface, inverse, axis=1), (0, 2, 1)))

    def one_bin(item):
        energy, speeds = item
        return advect_bin(energy, speeds[0], speeds[1], cur, wave_wet)

    advected = lax.map(one_bin, (spectrum, jnp.transpose(group_speed)))

    def one_row(row):
        first = jnp.take(row, pair_bins[0], axis=0).astype(jnp.float32)
        second = jnp.take(row, pair_bins[1], axis=0).astype(jnp.float32)
        products = (pair_coef[:, None] * first * second).astype(jnp.bfloat16)
        source = jax.ops.segment_sum(products.astype(jnp.float32), pair_bins[2], num_segments=NBINS)
        return (row.astype(jnp.float32) + DT_SOURCE * source).astype(jnp.bfloat16)

    rows_first = jnp.transpose(advected, (1, 0, 2))
    new_rows = lax.map(one_row, rows_first)
    new_spectrum = jnp.transpose(new_rows, (1, 0, 2))
    return new_spectrum, new_currents
```

```python
import functools
import jax
import jax.numpy as jnp
from jax import lax
from jax.experimental import pallas as pl
from jax.experimental.pallas import tpu as pltpu
from jax.sharding import PartitionSpec as P

DT_OCEAN = 0.5
CORIOLIS = 0.8
MIXING = 0.4
CURRENT_SCALE = 0.15
DT_SOURCE = 0.5


def shifted(value, axis, steps):
    count = lax.axis_size(axis)
    first, last = (max(0, -steps), min(count, count - steps))
    return lax.ppermute(value, axis, [(source, source + steps) for source in range(first, last)])


def levels_laplacian(field):
    upper = jnp.concatenate([field[..., :1], field[..., :-1]], axis=-1)
    lower = jnp.concatenate([field[..., 1:], field[..., -1:]], axis=-1)
    return upper + lower - 2.0 * field


def ocean_step(currents, drift, wet, levels):
    east = currents[..., :levels]
    north = currents[..., levels:]
    east_drift = drift[..., :levels]
    north_drift = drift[..., levels:]
    new_east = east + DT_OCEAN * (
        CORIOLIS * (north + north_drift) + MIXING * levels_laplacian(east)
    )
    new_north = north + DT_OCEAN * (
        -CORIOLIS * (east + east_drift) + MIXING * levels_laplacian(north)
    )
    return wet[..., None].astype(jnp.float32) * jnp.concatenate([new_east, new_north], axis=-1)


def advect_block(ext, speed_x, speed_y, cur, wet, columns):
    width = ext.shape[1] - 2 * columns
    energy = ext.astype(jnp.float32)
    cx = speed_x + cur[0:1, :]
    plus_x = jnp.maximum(cx, 0.0) * energy
    minus_x = jnp.minimum(cx, 0.0) * energy
    mid = slice(columns, columns + width)
    moved = energy[:, mid] - plus_x[:, mid] + plus_x[:, :width]
    moved = moved - minus_x[:, 2 * columns :] + minus_x[:, mid]
    cy = speed_y + cur[1:2, :]
    plus_y = jnp.maximum(cy, 0.0) * energy
    minus_y = jnp.minimum(cy, 0.0) * energy
    y = lax.rem(lax.broadcasted_iota(jnp.int32, (1, width), 1), columns)
    plus_prev = jnp.where(y == 0, 0.0, plus_y[:, columns - 1 : columns - 1 + width])
    minus_next = jnp.where(y == columns - 1, 0.0, minus_y[:, columns + 1 : columns + 1 + width])
    moved = moved - plus_y[:, mid] + plus_prev - minus_next + minus_y[:, mid]
    return (wet * moved).astype(jnp.bfloat16)


def wave_kernel(columns, chunk, ext_ref, speeds_ref, cur_ref, wet_ref, ids_ref, coef_ref, out_ref, adv, adv_t, total):
    step = pl.program_id(0)
    bins = adv.shape[0]

    @pl.when(step == 0)
    def _():
        cur = cur_ref[...]
        wet = wet_ref[...]

        def one(i, carry):
            rows = pl.ds(pl.multiple_of(i * chunk, chunk), chunk)
            speeds = speeds_ref[rows, :]
            adv[rows, :] = advect_block(
                ext_ref[rows, :], speeds[:, 0:1], speeds[:, 1:2], cur, wet, columns
            )
            return carry

        lax.fori_loop(0, bins // chunk, one, 0)
        adv_t[...] = adv[...].T
        total[...] = jnp.zeros_like(total)

    block = ids_ref.shape[1]
    bin_ids = lax.broadcasted_iota(jnp.int32, (bins, block), 0)

    def onehot(which):
        return jnp.where(bin_ids == ids_ref[which : which + 1, :], 1.0, 0.0).astype(jnp.bfloat16)

    first = jnp.dot(adv_t[...], onehot(0), preferred_element_type=jnp.float32)
    second = jnp.dot(adv_t[...], onehot(1), preferred_element_type=jnp.float32)
    products = (coef_ref[...] * first * second).astype(jnp.bfloat16)
    total[...] += lax.dot_general(
        onehot(2), products, (((1,), (1,)), ((), ())), preferred_element_type=jnp.float32
    )

    @pl.when(step == pl.num_programs(0) - 1)
    def _():
        out_ref[...] = (adv[...].astype(jnp.float32) + DT_SOURCE * total[...]).astype(jnp.bfloat16)


def wave_step(ext, speeds, cur, wet, pair_bins, pair_coef, columns):
    bins, wide = ext.shape
    width = wide - 2 * columns
    pairs = pair_bins.shape[1]
    block = 512 if pairs % 512 == 0 else pairs
    whole = lambda shape: pl.BlockSpec(shape, lambda i: (0, 0))
    chunk = 32 if bins % 32 == 0 else bins
    return pl.pallas_call(
        functools.partial(wave_kernel, columns, chunk),
        grid=(pairs // block,),
        out_shape=jax.ShapeDtypeStruct((bins, width), jnp.bfloat16),
        in_specs=[
            whole((bins, wide)),
            whole((bins, 2)),
            whole((2, wide)),
            whole((1, width)),
            pl.BlockSpec((3, block), lambda i: (0, i)),
            pl.BlockSpec((1, block), lambda i: (0, i)),
        ],
        out_specs=whole((bins, width)),
        scratch_shapes=[
            pltpu.VMEM((bins, width), jnp.bfloat16),
            pltpu.VMEM((width, bins), jnp.bfloat16),
            pltpu.VMEM((bins, width), jnp.float32),
        ],
        compiler_params=pltpu.CompilerParams(vmem_limit_bytes=48 * 1024 * 1024),
        cost_estimate=pl.CostEstimate(
            flops=6 * pairs * bins * width, bytes_accessed=4 * bins * wide, transcendentals=0
        ),
        name="wave_step",
    )(ext, speeds, cur, wet, pair_bins, pair_coef[None, :])


def per_device(
    spectrum,
    group_speed,
    stokes_kernel,
    pair_bins,
    pair_coef,
    currents,
    col_map,
    wave_wet,
    ocean_wet,
):
    local_bins, tile_rows, columns = spectrum.shape
    space_count = lax.axis_size("space")
    bins_count = lax.axis_size("bins")
    groups = space_count * bins_count
    group_cols = columns // groups
    levels = stokes_kernel.shape[1] // 2
    block_rows = tile_rows // bins_count
    width = block_rows * columns
    me = lax.axis_index("space") * bins_count + lax.axis_index("bins")
    slot_col = (
        col_map[:, None] * group_cols + jnp.arange(group_cols, dtype=jnp.int32)[None, :]
    ).reshape(-1)

    wet_f = ocean_wet.astype(jnp.float32)
    u0, u1 = currents[:, :, 0], currents[:, :, 1]
    v0, v1 = currents[:, :, levels], currents[:, :, levels + 1]
    su = wet_f * (u0 + DT_OCEAN * (CORIOLIS * v0 + MIXING * (u1 - u0)))
    sv = wet_f * (v0 + DT_OCEAN * (-CORIOLIS * u0 + MIXING * (v1 - v0)))
    surface = lax.all_gather(
        jnp.stack([su, sv, wet_f], axis=1), ("space", "bins"), axis=0, tiled=True
    )

    sending = jnp.transpose(spectrum.reshape(local_bins, bins_count, width), (1, 0, 2))
    flat = lax.all_to_all(sending, "bins", split_axis=0, concat_axis=0, tiled=True)
    flat = flat.reshape(bins_count * local_bins, width)
    below = shifted(flat[:, width - columns :], ("space", "bins"), 1)
    above = shifted(flat[:, :columns], ("space", "bins"), -1)
    ext = jnp.concatenate([below, flat, above], axis=1)

    speed_hi = group_speed.astype(jnp.bfloat16)
    speed_lo = (group_speed - speed_hi.astype(jnp.float32)).astype(jnp.bfloat16)
    tables = jnp.concatenate([stokes_kernel, speed_hi.T, speed_lo.T], axis=1)
    tables = lax.all_gather(tables, "bins", axis=0, tiled=True)
    kernel_all = tables[:, : 2 * levels]
    speeds = tables[:, 2 * levels :].astype(jnp.float32)
    speeds = speeds[:, 0:2] + speeds[:, 2:4]

    drift_cells = lax.dot_general(
        ext, kernel_all, (((0,), (0,)), ((), ())), preferred_element_type=jnp.float32
    )
    padded = jnp.pad(surface, ((0, 0), (0, 0), (1, 1)))
    mine = lax.dynamic_slice_in_dim(padded, me * block_rows, block_rows + 2, 2)
    here = slot_col[:, None] == jnp.arange(columns, dtype=jnp.int32)[None, :]
    mine = jnp.sum(jnp.where(here[:, None, None, :], mine[:, :, :, None], 0.0), axis=0)
    mine = mine.reshape(3, (block_rows + 2) * columns)
    half = DT_OCEAN * CORIOLIS
    cur = CURRENT_SCALE * jnp.tanh(
        jnp.stack(
            [
                mine[0] + half * mine[2] * drift_cells[:, levels],
                mine[1] - half * mine[2] * drift_cells[:, 0],
            ]
        )
    )
    wet_rows = lax.dynamic_slice_in_dim(
        wave_wet, lax.axis_index("bins") * block_rows, block_rows, 0
    )
    wet_rows = wet_rows.astype(jnp.float32).reshape(1, width)

    inner = drift_cells[columns : columns + width].reshape(block_rows, columns, 2 * levels)
    routed = jnp.einsum(
        "jc,xcl->jxl",
        here.astype(jnp.bfloat16),
        inner.astype(jnp.bfloat16),
        preferred_element_type=jnp.float32,
    ).astype(jnp.bfloat16)
    drift = lax.all_to_all(
        routed, ("space", "bins"), split_axis=0, concat_axis=1, tiled=True
    ).astype(jnp.float32)
    new_currents = ocean_step(currents, drift, ocean_wet, levels)

    updated = wave_step(ext, speeds, cur, wet_rows, pair_bins, pair_coef, columns)
    new_spectrum = updated.reshape(bins_count * local_bins, block_rows, columns)
    return (new_spectrum, new_currents)


def solution(mesh):
    placed = (
        P("bins", "space", None),
        P(None, "bins"),
        P("bins", None),
        P(),
        P(),
        P(("space", "bins"), None, None),
        P(),
        P("space", None),
        P(("space", "bins"), None),
    )
    return jax.shard_map(
        per_device,
        mesh=mesh,
        in_specs=placed,
        out_specs=(P(None, ("space", "bins"), None), P(("space", "bins"), None, None)),
        check_vma=False,
    )
```

```python
import functools
import jax
import jax.numpy as jnp
from jax import lax
from jax.experimental import pallas as pl
from jax.experimental.pallas import tpu as pltpu
from jax.sharding import PartitionSpec as P

DT_OCEAN = 0.5
CORIOLIS = 0.8
MIXING = 0.4
CURRENT_SCALE = 0.15
DT_SOURCE = 0.5


def exchange_kernel(
    space_count,
    bins_count,
    windows,
    table,
    speeds,
    edges,
    surface,
    windows_out,
    table_out,
    speeds_out,
    edges_out,
    surface_out,
    own_sem,
    send_sem,
    recv_sem,
    edge_send,
    edge_recv,
    surface_send,
    surface_recv,
):
    space, part = lax.axis_index("space"), lax.axis_index("bins")
    total = space_count * bins_count
    me = space * bins_count + part
    local_bins = table.shape[0]
    mine = pl.ds(pl.multiple_of(part * local_bins, 32), local_bins)

    def place(other):
        return (other // bins_count, lax.rem(other, bins_count))

    def remote(source, target, sent, received, device):
        return pltpu.make_async_remote_copy(
            src_ref=source,
            dst_ref=target,
            send_sem=sent,
            recv_sem=received,
            device_id=device,
            device_id_type=pl.DeviceIdType.MESH,
        )

    own = [
        pltpu.make_async_copy(windows.at[part], windows_out.at[mine, :], own_sem.at[0]),
        pltpu.make_async_copy(table, table_out.at[mine, :], own_sem.at[1]),
        pltpu.make_async_copy(speeds, speeds_out.at[part], own_sem.at[2]),
        pltpu.make_async_copy(surface.at[me], surface_out.at[me], own_sem.at[3]),
    ]
    for copy in own:
        copy.start()

    barrier = pltpu.get_barrier_semaphore()

    def greet(k, carry):
        pl.semaphore_signal(
            barrier,
            inc=1,
            device_id=place(lax.rem(me + k, total)),
            device_id_type=pl.DeviceIdType.MESH,
        )
        return carry

    lax.fori_loop(1, total, greet, 0)
    pl.semaphore_wait(barrier, total - 1)

    sends = []
    for j in range(1, bins_count):
        peer = lax.rem(part + j, bins_count)
        device = (space, peer)
        sends.append(
            remote(speeds, speeds_out.at[part], send_sem.at[0, j], recv_sem.at[0, j], device)
        )
        sends.append(
            remote(table, table_out.at[mine, :], send_sem.at[1, j], recv_sem.at[1, j], device)
        )
        sends.append(
            remote(
                windows.at[peer],
                windows_out.at[mine, :],
                send_sem.at[2, j],
                recv_sem.at[2, j],
                device,
            )
        )
    for copy in sends:
        copy.start()

    def up():
        return remote(
            edges.at[0],
            edges_out.at[mine, :],
            edge_send.at[0],
            edge_recv.at[part],
            (space + 1, 0),
        )

    def down():
        return remote(
            edges.at[1],
            edges_out.at[mine, :],
            edge_send.at[1],
            edge_recv.at[part],
            (space - 1, bins_count - 1),
        )

    pl.when(space < space_count - 1)(lambda: up().start())
    pl.when(space > 0)(lambda: down().start())

    def to_other(k):
        other = lax.rem(me + k, total)
        return remote(
            surface.at[other],
            surface_out.at[me],
            surface_send.at[k],
            surface_recv.at[k],
            place(other),
        )

    def start_one(k, carry):
        to_other(k).start()
        return carry

    def finish_one(k, carry):
        to_other(k).wait()
        return carry

    lax.fori_loop(1, total, start_one, 0)
    lax.fori_loop(1, total, finish_one, 0)
    pl.when(space < space_count - 1)(lambda: up().wait_send())
    pl.when(space > 0)(lambda: down().wait_send())

    def arrive(which):
        rows = pl.ds(which * local_bins, local_bins)
        remote(
            edges.at[0], edges_out.at[rows, :], edge_send.at[0], edge_recv.at[which], (space, part)
        ).wait_recv()

    def arrive_all():
        for which in range(bins_count):
            arrive(which)

    pl.when((part == 0) & (space > 0))(arrive_all)
    pl.when((part == bins_count - 1) & (space < space_count - 1))(arrive_all)
    for copy in sends:
        copy.wait()
    for copy in own:
        copy.wait()


def exchange(windows, table, speeds, edges, surface, space_count, bins_count):
    anywhere = pl.BlockSpec(memory_space=pl.ANY)
    local_bins = table.shape[0]
    bins = local_bins * bins_count
    total = space_count * bins_count
    dma = pltpu.SemaphoreType.DMA
    return pl.pallas_call(
        functools.partial(exchange_kernel, space_count, bins_count),
        out_shape=(
            jax.ShapeDtypeStruct((bins, windows.shape[2]), windows.dtype),
            jax.ShapeDtypeStruct((bins, table.shape[1]), table.dtype),
            jax.ShapeDtypeStruct((bins_count,) + speeds.shape, speeds.dtype),
            jax.ShapeDtypeStruct((bins, edges.shape[2]), edges.dtype),
            jax.ShapeDtypeStruct(surface.shape, surface.dtype),
        ),
        in_specs=[anywhere] * 5,
        out_specs=(anywhere,) * 5,
        scratch_shapes=[
            dma((4,)),
            dma((3, bins_count)),
            dma((3, bins_count)),
            dma((2,)),
            dma((bins_count,)),
            dma((total,)),
            dma((total,)),
        ],
        compiler_params=pltpu.CompilerParams(collective_id=0, has_side_effects=True),
        name="exchange",
    )(windows, table, speeds, edges, surface)


def levels_laplacian(field):
    upper = jnp.concatenate([field[..., :1], field[..., :-1]], axis=-1)
    lower = jnp.concatenate([field[..., 1:], field[..., -1:]], axis=-1)
    return upper + lower - 2.0 * field


def ocean_step(currents, drift, wet, levels):
    east = currents[..., :levels]
    north = currents[..., levels:]
    east_drift = drift[..., :levels]
    north_drift = drift[..., levels:]
    new_east = east + DT_OCEAN * (
        CORIOLIS * (north + north_drift) + MIXING * levels_laplacian(east)
    )
    new_north = north + DT_OCEAN * (
        -CORIOLIS * (east + east_drift) + MIXING * levels_laplacian(north)
    )
    return wet[..., None].astype(jnp.float32) * jnp.concatenate([new_east, new_north], axis=-1)


def advect_block(ext, speed_x, speed_y, cur, wet, columns):
    width = ext.shape[1] - 2 * columns
    energy = ext
    cx = speed_x + cur[0:1, :]
    plus_x = jnp.maximum(cx, 0.0) * energy
    minus_x = jnp.minimum(cx, 0.0) * energy
    mid = slice(columns, columns + width)
    moved = energy[:, mid] - plus_x[:, mid] + plus_x[:, :width]
    moved = moved - minus_x[:, 2 * columns :] + minus_x[:, mid]
    cy = speed_y + cur[1:2, :]
    plus_y = jnp.maximum(cy, 0.0) * energy
    minus_y = jnp.minimum(cy, 0.0) * energy
    y = lax.rem(lax.broadcasted_iota(jnp.int32, (1, width), 1), columns)
    plus_prev = jnp.where(y == 0, 0.0, plus_y[:, columns - 1 : columns - 1 + width])
    minus_next = jnp.where(y == columns - 1, 0.0, minus_y[:, columns + 1 : columns + 1 + width])
    moved = moved - plus_y[:, mid] + plus_prev - minus_next + minus_y[:, mid]
    return (wet * moved).astype(jnp.bfloat16)


def wave_kernel(columns, chunk, win_ref, near_ref, speeds_ref, cur_ref, wet_ref, ids_ref, coef_ref, out_ref, adv, adv_t, total):
    step = pl.program_id(0)
    bins = adv.shape[0]

    @pl.when(step == 0)
    def _():
        cur = cur_ref[...]
        wet = wet_ref[...]

        def one(i, carry):
            rows = pl.ds(pl.multiple_of(i * chunk, chunk), chunk)
            speeds = speeds_ref[rows, :]
            near = near_ref[rows, :].astype(jnp.float32)
            main = win_ref[rows, 2 * columns :].astype(jnp.float32)
            ext = jnp.concatenate([near[:, :columns], main, near[:, columns:]], axis=1)
            adv[rows, :] = advect_block(
                ext, speeds[:, 0:1], speeds[:, 1:2], cur, wet, columns
            )
            return carry

        lax.fori_loop(0, bins // chunk, one, 0)
        adv_t[...] = adv[...].T
        total[...] = jnp.zeros_like(total)

    block = ids_ref.shape[1]
    bin_ids = lax.broadcasted_iota(jnp.int32, (bins, block), 0)

    def onehot(which):
        return jnp.where(bin_ids == ids_ref[which : which + 1, :], 1.0, 0.0).astype(jnp.bfloat16)

    first = jnp.dot(adv_t[...], onehot(0), preferred_element_type=jnp.float32)
    second = jnp.dot(adv_t[...], onehot(1), preferred_element_type=jnp.float32)
    products = (coef_ref[...] * first * second).astype(jnp.bfloat16)
    total[...] += lax.dot_general(
        onehot(2), products, (((1,), (1,)), ((), ())), preferred_element_type=jnp.float32
    )

    @pl.when(step == pl.num_programs(0) - 1)
    def _():
        out_ref[...] = (adv[...].astype(jnp.float32) + DT_SOURCE * total[...]).astype(jnp.bfloat16)


def wave_step(win, near, speeds, cur, wet, pair_bins, pair_coef, columns):
    bins, wide = win.shape
    width = wide - 2 * columns
    pairs = pair_bins.shape[1]
    block = 512 if pairs % 512 == 0 else pairs
    whole = lambda shape: pl.BlockSpec(shape, lambda i: (0, 0))
    chunk = 32 if bins % 32 == 0 else bins
    return pl.pallas_call(
        functools.partial(wave_kernel, columns, chunk),
        grid=(pairs // block,),
        out_shape=jax.ShapeDtypeStruct((bins, width), jnp.bfloat16),
        in_specs=[
            whole((bins, wide)),
            whole((bins, 2 * columns)),
            whole((bins, 2)),
            whole((2, wide)),
            whole((1, width)),
            pl.BlockSpec((3, block), lambda i: (0, i)),
            pl.BlockSpec((1, block), lambda i: (0, i)),
        ],
        out_specs=whole((bins, width)),
        scratch_shapes=[
            pltpu.VMEM((bins, width), jnp.bfloat16),
            pltpu.VMEM((width, bins), jnp.bfloat16),
            pltpu.VMEM((bins, width), jnp.float32),
        ],
        compiler_params=pltpu.CompilerParams(vmem_limit_bytes=48 * 1024 * 1024),
        cost_estimate=pl.CostEstimate(
            flops=6 * pairs * bins * width, bytes_accessed=4 * bins * wide, transcendentals=0
        ),
        name="wave_step",
    )(win, near, speeds, cur, wet, pair_bins, pair_coef[None, :])


def per_device(
    spectrum,
    group_speed,
    stokes_kernel,
    pair_bins,
    pair_coef,
    currents,
    col_map,
    wave_wet,
    ocean_wet,
):
    local_bins, tile_rows, columns = spectrum.shape
    space_count = lax.axis_size("space")
    bins_count = lax.axis_size("bins")
    groups = space_count * bins_count
    group_cols = columns // groups
    levels = stokes_kernel.shape[1] // 2
    block_rows = tile_rows // bins_count
    width = block_rows * columns
    slot_col = (
        col_map[:, None] * group_cols + jnp.arange(group_cols, dtype=jnp.int32)[None, :]
    ).reshape(-1)

    wet_f = ocean_wet.astype(jnp.float32)
    u0, u1 = currents[:, :, 0], currents[:, :, 1]
    v0, v1 = currents[:, :, levels], currents[:, :, levels + 1]
    su = wet_f * (u0 + DT_OCEAN * (CORIOLIS * v0 + MIXING * (u1 - u0)))
    sv = wet_f * (v0 + DT_OCEAN * (-CORIOLIS * u0 + MIXING * (v1 - v0)))
    surface = jnp.stack([su, sv, wet_f])

    def windows_of(rows, before, after):
        before = jnp.concatenate([before, rows[..., :-1, -1:]], axis=-2)
        after = jnp.concatenate([rows[..., 1:, :1], after], axis=-2)
        return jnp.concatenate([before, after, rows], axis=-1)

    none = jnp.zeros((3, group_cols, 1, 1), jnp.float32)
    surface = windows_of(
        surface.reshape(3, group_cols, groups, block_rows), none, none
    )
    window_rows = block_rows + 2
    surface = jnp.transpose(surface, (2, 0, 1, 3)).reshape(groups, 1, 3 * group_cols * window_rows)
    used = surface.shape[2]
    surface = jnp.pad(surface, ((0, 0), (0, 0), (0, -used % 128)))

    rows = spectrum.reshape(local_bins, bins_count, width)
    zeros = jnp.zeros((local_bins, 1, columns), spectrum.dtype)
    before = jnp.concatenate([zeros, rows[:, :-1, width - columns :]], axis=1)
    after = jnp.concatenate([rows[:, 1:, :columns], zeros], axis=1)
    windows = jnp.transpose(jnp.concatenate([before, after, rows], axis=2), (1, 0, 2))
    zero = zeros[:, 0]
    edges = jnp.stack(
        [
            jnp.concatenate([spectrum[:, -1, :], zero], axis=1),
            jnp.concatenate([zero, spectrum[:, 0, :]], axis=1),
        ]
    )
    speeds = jnp.pad(group_speed, ((0, -2 % 8), (0, -local_bins % 128)))
    win, kernel_all, speeds, edges, surface = exchange(
        windows, stokes_kernel, speeds, edges, surface, space_count, bins_count
    )
    speeds = jnp.transpose(speeds[:, :2, :local_bins], (0, 2, 1)).reshape(-1, 2)
    space, part = lax.axis_index("space"), lax.axis_index("bins")
    from_below = (part == 0) & (space > 0)
    from_above = (part == bins_count - 1) & (space < space_count - 1)
    is_below = jnp.arange(2 * columns, dtype=jnp.int32) < columns
    take_edge = jnp.where(is_below, from_below, from_above)
    near = jnp.where(take_edge[None, :], edges, win[:, : 2 * columns])

    def project(cells):
        return lax.dot_general(
            cells, kernel_all, (((0,), (0,)), ((), ())), preferred_element_type=jnp.float32
        )

    drift_near, drift_main = project(near), project(win[:, 2 * columns :])

    def in_order(cells_near, cells_main):
        return jnp.concatenate([cells_near[:columns], cells_main, cells_near[columns:]])

    mine = surface[:, 0, :used].reshape(groups, 3, group_cols, window_rows)
    mine = jnp.transpose(mine, (0, 2, 1, 3)).reshape(groups * group_cols, 3, window_rows)
    here = slot_col[:, None] == jnp.arange(columns, dtype=jnp.int32)[None, :]
    mine = jnp.sum(jnp.where(here[:, None, None, :], mine[:, :, :, None], 0.0), axis=0)
    mine = jnp.concatenate([mine[:, :1], mine[:, 2:], mine[:, 1:2]], axis=1)
    mine = mine.reshape(3, window_rows * columns)
    half = DT_OCEAN * CORIOLIS
    cur = CURRENT_SCALE * jnp.tanh(
        jnp.stack(
            [
                mine[0] + half * mine[2] * in_order(drift_near[:, levels], drift_main[:, levels]),
                mine[1] - half * mine[2] * in_order(drift_near[:, 0], drift_main[:, 0]),
            ]
        )
    )
    wet_rows = lax.dynamic_slice_in_dim(
        wave_wet, lax.axis_index("bins") * block_rows, block_rows, 0
    )
    wet_rows = wet_rows.astype(jnp.float32).reshape(1, width)

    inner = drift_main.reshape(block_rows, columns, 2 * levels)
    routed = jnp.einsum(
        "jc,xcl->jxl",
        here.astype(jnp.bfloat16),
        inner.astype(jnp.bfloat16),
        preferred_element_type=jnp.float32,
    ).astype(jnp.bfloat16)
    drift = lax.all_to_all(
        routed, ("space", "bins"), split_axis=0, concat_axis=1, tiled=True
    ).astype(jnp.float32)
    new_currents = ocean_step(currents, drift, ocean_wet, levels)

    updated = wave_step(win, near, speeds, cur, wet_rows, pair_bins, pair_coef, columns)
    new_spectrum = updated.reshape(bins_count * local_bins, block_rows, columns)
    return (new_spectrum, new_currents)


def solution(mesh):
    placed = (
        P("bins", "space", None),
        P(None, "bins"),
        P("bins", None),
        P(),
        P(),
        P(("space", "bins"), None, None),
        P(),
        P("space", None),
        P(("space", "bins"), None),
    )
    return jax.shard_map(
        per_device,
        mesh=mesh,
        in_specs=placed,
        out_specs=(P(None, ("space", "bins"), None), P(("space", "bins"), None, None)),
        check_vma=False,
    )
```

```python
import functools
import jax
import jax.numpy as jnp
from jax import lax
from jax.experimental import pallas as pl
from jax.experimental.pallas import tpu as pltpu
from jax.sharding import PartitionSpec as P

DT_OCEAN = 0.5
CORIOLIS = 0.8
MIXING = 0.4
CURRENT_SCALE = 0.15
DT_SOURCE = 0.5


def exchange_kernel(
    space_count,
    bins_count,
    windows,
    table,
    speeds,
    edges,
    surface,
    windows_out,
    table_out,
    speeds_out,
    edges_out,
    surface_out,
    own_sem,
    send_sem,
    recv_sem,
    edge_send,
    edge_recv,
    surface_send,
    surface_recv,
):
    space, part = lax.axis_index("space"), lax.axis_index("bins")
    total = space_count * bins_count
    me = space * bins_count + part
    local_bins = table.shape[0]
    mine = pl.ds(pl.multiple_of(part * local_bins, 32), local_bins)

    def place(other):
        return (other // bins_count, lax.rem(other, bins_count))

    def remote(source, target, sent, received, device):
        return pltpu.make_async_remote_copy(
            src_ref=source,
            dst_ref=target,
            send_sem=sent,
            recv_sem=received,
            device_id=device,
            device_id_type=pl.DeviceIdType.MESH,
        )

    own = [
        pltpu.make_async_copy(windows.at[part], windows_out.at[mine, :], own_sem.at[0]),
        pltpu.make_async_copy(table, table_out.at[mine, :], own_sem.at[1]),
        pltpu.make_async_copy(speeds, speeds_out.at[part], own_sem.at[2]),
        pltpu.make_async_copy(surface.at[me], surface_out.at[me], own_sem.at[3]),
    ]
    for copy in own:
        copy.start()

    barrier = pltpu.get_barrier_semaphore()

    def greet(k, carry):
        pl.semaphore_signal(
            barrier,
            inc=1,
            device_id=place(lax.rem(me + k, total)),
            device_id_type=pl.DeviceIdType.MESH,
        )
        return carry

    lax.fori_loop(1, total, greet, 0)
    pl.semaphore_wait(barrier, total - 1)

    sends = []
    for j in range(1, bins_count):
        peer = lax.rem(part + j, bins_count)
        device = (space, peer)
        sends.append(
            remote(speeds, speeds_out.at[part], send_sem.at[0, j], recv_sem.at[0, j], device)
        )
        sends.append(
            remote(table, table_out.at[mine, :], send_sem.at[1, j], recv_sem.at[1, j], device)
        )
        sends.append(
            remote(
                windows.at[peer],
                windows_out.at[mine, :],
                send_sem.at[2, j],
                recv_sem.at[2, j],
                device,
            )
        )
    for copy in sends:
        copy.start()

    def up():
        return remote(
            edges.at[0],
            edges_out.at[mine, :],
            edge_send.at[0],
            edge_recv.at[part],
            (space + 1, 0),
        )

    def down():
        return remote(
            edges.at[1],
            edges_out.at[mine, :],
            edge_send.at[1],
            edge_recv.at[part],
            (space - 1, bins_count - 1),
        )

    pl.when(space < space_count - 1)(lambda: up().start())
    pl.when(space > 0)(lambda: down().start())

    def to_other(k):
        other = lax.rem(me + k, total)
        return remote(
            surface.at[other],
            surface_out.at[me],
            surface_send.at[k],
            surface_recv.at[k],
            place(other),
        )

    def start_one(k, carry):
        to_other(k).start()
        return carry

    def finish_one(k, carry):
        to_other(k).wait()
        return carry

    lax.fori_loop(1, total, start_one, 0)
    lax.fori_loop(1, total, finish_one, 0)
    pl.when(space < space_count - 1)(lambda: up().wait_send())
    pl.when(space > 0)(lambda: down().wait_send())

    def arrive(which):
        rows = pl.ds(which * local_bins, local_bins)
        remote(
            edges.at[0], edges_out.at[rows, :], edge_send.at[0], edge_recv.at[which], (space, part)
        ).wait_recv()

    def arrive_all():
        for which in range(bins_count):
            arrive(which)

    pl.when((part == 0) & (space > 0))(arrive_all)
    pl.when((part == bins_count - 1) & (space < space_count - 1))(arrive_all)
    for copy in sends:
        copy.wait()
    for copy in own:
        copy.wait()


def exchange(windows, table, speeds, edges, surface, space_count, bins_count):
    anywhere = pl.BlockSpec(memory_space=pl.ANY)
    local_bins = table.shape[0]
    bins = local_bins * bins_count
    total = space_count * bins_count
    dma = pltpu.SemaphoreType.DMA
    return pl.pallas_call(
        functools.partial(exchange_kernel, space_count, bins_count),
        out_shape=(
            jax.ShapeDtypeStruct((bins, windows.shape[2]), windows.dtype),
            jax.ShapeDtypeStruct((bins, table.shape[1]), table.dtype),
            jax.ShapeDtypeStruct((bins_count,) + speeds.shape, speeds.dtype),
            jax.ShapeDtypeStruct((bins, edges.shape[2]), edges.dtype),
            jax.ShapeDtypeStruct(surface.shape, surface.dtype),
        ),
        in_specs=[anywhere] * 5,
        out_specs=(anywhere,) * 5,
        scratch_shapes=[
            dma((4,)),
            dma((3, bins_count)),
            dma((3, bins_count)),
            dma((2,)),
            dma((bins_count,)),
            dma((total,)),
            dma((total,)),
        ],
        compiler_params=pltpu.CompilerParams(collective_id=0, has_side_effects=True),
        name="exchange",
    )(windows, table, speeds, edges, surface)


def levels_laplacian(field):
    upper = jnp.concatenate([field[..., :1], field[..., :-1]], axis=-1)
    lower = jnp.concatenate([field[..., 1:], field[..., -1:]], axis=-1)
    return upper + lower - 2.0 * field


def ocean_step(currents, drift, wet, levels):
    east = currents[..., :levels]
    north = currents[..., levels:]
    east_drift = drift[..., :levels]
    north_drift = drift[..., levels:]
    new_east = east + DT_OCEAN * (
        CORIOLIS * (north + north_drift) + MIXING * levels_laplacian(east)
    )
    new_north = north + DT_OCEAN * (
        -CORIOLIS * (east + east_drift) + MIXING * levels_laplacian(north)
    )
    return wet[..., None].astype(jnp.float32) * jnp.concatenate([new_east, new_north], axis=-1)


def advect_block(energy, speeds, cur_x, cur_y, wet, columns):
    cells = energy.shape[0] - 2 * columns
    mid = slice(columns, columns + cells)
    cx = speeds[0:1, :] + cur_x
    from_before = jnp.maximum(cx[:cells], 0.0) * energy[:cells]
    from_after = jnp.minimum(cx[2 * columns :], 0.0) * energy[2 * columns :]
    own = energy[mid]
    cy = speeds[1:2, :] + cur_y[mid]
    plus = jnp.maximum(cy, 0.0) * own
    minus = jnp.minimum(cy, 0.0) * own
    y = lax.rem(lax.broadcasted_iota(jnp.int32, own.shape, 0), columns)
    plus_prev = jnp.where(y == 0, 0.0, pltpu.roll(plus, 1, 0))
    minus_next = jnp.where(y == columns - 1, 0.0, pltpu.roll(minus, cells - 1, 0))
    moved = own - (jnp.abs(cx[mid]) + jnp.abs(cy)) * own
    moved = moved + from_before - from_after + plus_prev - minus_next
    return (wet * moved).astype(jnp.bfloat16)


def wave_kernel(
    columns,
    chunk,
    win_ref,
    edges_ref,
    mask_ref,
    kernel_ref,
    speeds_ref,
    surface_ref,
    wet_ref,
    ids_ref,
    coef_ref,
    out_ref,
    ext,
    cur,
    wet,
    adv,
    total,
):
    step = pl.program_id(0)
    cells, bins = adv.shape
    levels = kernel_ref.shape[1] // 2

    @pl.when(step == 0)
    def _():
        take_edge = mask_ref[...] > 0.0

        def turn(i, carry):
            rows = pl.ds(pl.multiple_of(i * chunk, chunk), chunk)
            near = win_ref[rows, : 2 * columns].astype(jnp.float32)
            near = jnp.where(take_edge, edges_ref[rows, :].astype(jnp.float32), near).T
            main = win_ref[rows, 2 * columns :].astype(jnp.float32).T
            ext[:columns, rows] = near[:columns].astype(jnp.bfloat16)
            ext[columns : columns + cells, rows] = main.astype(jnp.bfloat16)
            ext[columns + cells :, rows] = near[columns:].astype(jnp.bfloat16)
            return carry

        lax.fori_loop(0, bins // chunk, turn, 0)
        drift = jnp.dot(ext[...], kernel_ref[...], preferred_element_type=jnp.float32)
        half = DT_OCEAN * CORIOLIS

        def wide(row):
            return jnp.broadcast_to(row, (chunk, row.shape[1])).T

        weight = half * wide(surface_ref[2:3, :])
        cur[0] = CURRENT_SCALE * jnp.tanh(
            wide(surface_ref[0:1, :]) + weight * drift[:, levels : levels + 1]
        )
        cur[1] = CURRENT_SCALE * jnp.tanh(
            wide(surface_ref[1:2, :]) - weight * drift[:, 0:1]
        )
        wet[...] = wide(wet_ref[...])

        def one(i, carry):
            lanes = pl.ds(pl.multiple_of(i * chunk, chunk), chunk)
            adv[:, lanes] = advect_block(
                ext[:, lanes].astype(jnp.float32),
                speeds_ref[:, lanes],
                cur[0],
                cur[1],
                wet[...],
                columns,
            )
            return carry

        lax.fori_loop(0, bins // chunk, one, 0)
        total[...] = jnp.zeros_like(total)

    block = ids_ref.shape[1]
    bin_ids = lax.broadcasted_iota(jnp.int32, (bins, block), 0)

    def onehot(which):
        return jnp.where(bin_ids == ids_ref[which : which + 1, :], 1.0, 0.0).astype(jnp.bfloat16)

    first = jnp.dot(adv[...], onehot(0), preferred_element_type=jnp.float32)
    second = jnp.dot(adv[...], onehot(1), preferred_element_type=jnp.float32)
    products = (coef_ref[...] * first * second).astype(jnp.bfloat16)
    total[...] += lax.dot_general(
        products, onehot(2), (((1,), (1,)), ((), ())), preferred_element_type=jnp.float32
    )

    @pl.when(step == pl.num_programs(0) - 1)
    def _():
        out_ref[...] = (adv[...].astype(jnp.float32) + DT_SOURCE * total[...]).astype(jnp.bfloat16)


def wave_step(win, edges, mask, kernel_all, speeds, surface, wet, pair_bins, pair_coef, columns):
    bins, wide = win.shape
    cells = wide - 2 * columns
    pairs = pair_bins.shape[1]
    block = 512 if pairs % 512 == 0 else pairs
    chunk = 128 if bins % 128 == 0 else bins
    whole = lambda shape: pl.BlockSpec(shape, lambda i: (0, 0))
    return pl.pallas_call(
        functools.partial(wave_kernel, columns, chunk),
        grid=(pairs // block,),
        out_shape=jax.ShapeDtypeStruct((cells, bins), jnp.bfloat16),
        in_specs=[
            whole(win.shape),
            whole(edges.shape),
            whole(mask.shape),
            whole(kernel_all.shape),
            whole(speeds.shape),
            whole(surface.shape),
            whole(wet.shape),
            pl.BlockSpec((3, block), lambda i: (0, i)),
            pl.BlockSpec((1, block), lambda i: (0, i)),
        ],
        out_specs=whole((cells, bins)),
        scratch_shapes=[
            pltpu.VMEM((wide, bins), jnp.bfloat16),
            pltpu.VMEM((2, wide, chunk), jnp.float32),
            pltpu.VMEM((cells, chunk), jnp.float32),
            pltpu.VMEM((cells, bins), jnp.bfloat16),
            pltpu.VMEM((cells, bins), jnp.float32),
        ],
        compiler_params=pltpu.CompilerParams(vmem_limit_bytes=48 * 1024 * 1024),
        cost_estimate=pl.CostEstimate(
            flops=6 * pairs * bins * cells, bytes_accessed=4 * bins * wide, transcendentals=0
        ),
        name="wave_step",
    )(win, edges, mask, kernel_all, speeds, surface, wet, pair_bins, pair_coef[None, :])


def per_device(
    spectrum,
    group_speed,
    stokes_kernel,
    pair_bins,
    pair_coef,
    currents,
    col_map,
    wave_wet,
    ocean_wet,
):
    local_bins, tile_rows, columns = spectrum.shape
    space_count = lax.axis_size("space")
    bins_count = lax.axis_size("bins")
    groups = space_count * bins_count
    group_cols = columns // groups
    levels = stokes_kernel.shape[1] // 2
    block_rows = tile_rows // bins_count
    width = block_rows * columns
    slot_col = (
        col_map[:, None] * group_cols + jnp.arange(group_cols, dtype=jnp.int32)[None, :]
    ).reshape(-1)

    wet_f = ocean_wet.astype(jnp.float32)
    u0, u1 = currents[:, :, 0], currents[:, :, 1]
    v0, v1 = currents[:, :, levels], currents[:, :, levels + 1]
    su = wet_f * (u0 + DT_OCEAN * (CORIOLIS * v0 + MIXING * (u1 - u0)))
    sv = wet_f * (v0 + DT_OCEAN * (-CORIOLIS * u0 + MIXING * (v1 - v0)))
    surface = jnp.stack([su, sv, wet_f])

    def windows_of(rows, before, after):
        before = jnp.concatenate([before, rows[..., :-1, -1:]], axis=-2)
        after = jnp.concatenate([rows[..., 1:, :1], after], axis=-2)
        return jnp.concatenate([before, after, rows], axis=-1)

    none = jnp.zeros((3, group_cols, 1, 1), jnp.float32)
    surface = windows_of(
        surface.reshape(3, group_cols, groups, block_rows), none, none
    )
    window_rows = block_rows + 2
    surface = jnp.transpose(surface, (2, 0, 1, 3)).reshape(groups, 1, 3 * group_cols * window_rows)
    used = surface.shape[2]
    surface = jnp.pad(surface, ((0, 0), (0, 0), (0, -used % 128)))

    rows = spectrum.reshape(local_bins, bins_count, width)
    zeros = jnp.zeros((local_bins, 1, columns), spectrum.dtype)
    before = jnp.concatenate([zeros, rows[:, :-1, width - columns :]], axis=1)
    after = jnp.concatenate([rows[:, 1:, :columns], zeros], axis=1)
    windows = jnp.transpose(jnp.concatenate([before, after, rows], axis=2), (1, 0, 2))
    zero = zeros[:, 0]
    edges = jnp.stack(
        [
            jnp.concatenate([spectrum[:, -1, :], zero], axis=1),
            jnp.concatenate([zero, spectrum[:, 0, :]], axis=1),
        ]
    )
    speeds = jnp.pad(group_speed, ((0, -2 % 8), (0, -local_bins % 128)))
    win, kernel_all, speeds, edges, surface = exchange(
        windows, stokes_kernel, speeds, edges, surface, space_count, bins_count
    )
    speeds = jnp.transpose(speeds[:, :2, :local_bins], (1, 0, 2)).reshape(2, -1)
    space, part = lax.axis_index("space"), lax.axis_index("bins")
    from_below = (part == 0) & (space > 0)
    from_above = (part == bins_count - 1) & (space < space_count - 1)
    is_below = jnp.arange(2 * columns, dtype=jnp.int32) < columns
    take_edge = jnp.where(is_below, from_below, from_above)
    take_edge = take_edge.astype(jnp.float32)[None, :]
    drift_main = lax.dot_general(
        win[:, 2 * columns :],
        kernel_all,
        (((0,), (0,)), ((), ())),
        preferred_element_type=jnp.float32,
    )
    mine = surface[:, 0, :used].reshape(groups, 3, group_cols, window_rows)
    mine = jnp.transpose(mine, (0, 2, 1, 3)).reshape(groups * group_cols, 3, window_rows)
    here = slot_col[:, None] == jnp.arange(columns, dtype=jnp.int32)[None, :]
    mine = jnp.sum(jnp.where(here[:, None, None, :], mine[:, :, :, None], 0.0), axis=0)
    mine = jnp.concatenate([mine[:, :1], mine[:, 2:], mine[:, 1:2]], axis=1)
    mine = mine.reshape(3, window_rows * columns)
    wet_rows = lax.dynamic_slice_in_dim(
        wave_wet, lax.axis_index("bins") * block_rows, block_rows, 0
    )
    wet_rows = wet_rows.astype(jnp.float32).reshape(1, width)

    inner = drift_main.reshape(block_rows, columns, 2 * levels)
    routed = jnp.einsum(
        "jc,xcl->jxl",
        here.astype(jnp.bfloat16),
        inner.astype(jnp.bfloat16),
        preferred_element_type=jnp.float32,
    ).astype(jnp.bfloat16)
    drift = lax.all_to_all(
        routed, ("space", "bins"), split_axis=0, concat_axis=1, tiled=True
    ).astype(jnp.float32)
    new_currents = ocean_step(currents, drift, ocean_wet, levels)

    updated = wave_step(
        win, edges, take_edge, kernel_all, speeds, mine, wet_rows, pair_bins, pair_coef, columns
    )
    new_spectrum = jnp.transpose(
        updated.reshape(block_rows, columns, bins_count * local_bins), (2, 0, 1)
    )
    return (new_spectrum, new_currents)


def solution(mesh):
    placed = (
        P("bins", "space", None),
        P(None, "bins"),
        P("bins", None),
        P(),
        P(),
        P(("space", "bins"), None, None),
        P(),
        P("space", None),
        P(("space", "bins"), None),
    )
    return jax.shard_map(
        per_device,
        mesh=mesh,
        in_specs=placed,
        out_specs=(P(None, ("space", "bins"), None), P(("space", "bins"), None, None)),
        check_vma=False,
    )
```

```python
import functools
import jax
import jax.numpy as jnp
from jax import lax
from jax.experimental import pallas as pl
from jax.experimental.pallas import tpu as pltpu
from jax.sharding import PartitionSpec as P

DT_OCEAN = 0.5
CORIOLIS = 0.8
MIXING = 0.4
CURRENT_SCALE = 0.15
DT_SOURCE = 0.5


def exchange_kernel(
    space_count,
    bins_count,
    windows,
    table,
    speeds,
    edges,
    surface,
    windows_out,
    table_out,
    speeds_out,
    edges_out,
    surface_out,
    own_sem,
    send_sem,
    recv_sem,
    edge_send,
    edge_recv,
    surface_send,
    surface_recv,
):
    space, part = lax.axis_index("space"), lax.axis_index("bins")
    total = space_count * bins_count
    me = space * bins_count + part
    local_bins = table.shape[0]
    mine = pl.ds(pl.multiple_of(part * local_bins, 32), local_bins)

    def place(other):
        return (other // bins_count, lax.rem(other, bins_count))

    def remote(source, target, sent, received, device):
        return pltpu.make_async_remote_copy(
            src_ref=source,
            dst_ref=target,
            send_sem=sent,
            recv_sem=received,
            device_id=device,
            device_id_type=pl.DeviceIdType.MESH,
        )

    own = [
        pltpu.make_async_copy(windows.at[part], windows_out.at[mine, :], own_sem.at[0]),
        pltpu.make_async_copy(table, table_out.at[mine, :], own_sem.at[1]),
        pltpu.make_async_copy(speeds, speeds_out.at[part], own_sem.at[2]),
        pltpu.make_async_copy(surface.at[me], surface_out.at[me], own_sem.at[3]),
    ]
    for copy in own:
        copy.start()

    barrier = pltpu.get_barrier_semaphore()

    def greet(k, carry):
        pl.semaphore_signal(
            barrier,
            inc=1,
            device_id=place(lax.rem(me + k, total)),
            device_id_type=pl.DeviceIdType.MESH,
        )
        return carry

    lax.fori_loop(1, total, greet, 0)
    pl.semaphore_wait(barrier, total - 1)

    sends = []
    for j in range(1, bins_count):
        peer = lax.rem(part + j, bins_count)
        device = (space, peer)
        sends.append(
            remote(speeds, speeds_out.at[part], send_sem.at[0, j], recv_sem.at[0, j], device)
        )
        sends.append(
            remote(table, table_out.at[mine, :], send_sem.at[1, j], recv_sem.at[1, j], device)
        )
        sends.append(
            remote(
                windows.at[peer],
                windows_out.at[mine, :],
                send_sem.at[2, j],
                recv_sem.at[2, j],
                device,
            )
        )
    for copy in sends:
        copy.start()

    def up():
        return remote(
            edges.at[0],
            edges_out.at[mine, :],
            edge_send.at[0],
            edge_recv.at[part],
            (space + 1, 0),
        )

    def down():
        return remote(
            edges.at[1],
            edges_out.at[mine, :],
            edge_send.at[1],
            edge_recv.at[part],
            (space - 1, bins_count - 1),
        )

    pl.when(space < space_count - 1)(lambda: up().start())
    pl.when(space > 0)(lambda: down().start())

    def to_other(k):
        other = lax.rem(me + k, total)
        return remote(
            surface.at[other],
            surface_out.at[me],
            surface_send.at[k],
            surface_recv.at[k],
            place(other),
        )

    def start_one(k, carry):
        to_other(k).start()
        return carry

    def finish_one(k, carry):
        to_other(k).wait()
        return carry

    lax.fori_loop(1, total, start_one, 0)
    lax.fori_loop(1, total, finish_one, 0)
    pl.when(space < space_count - 1)(lambda: up().wait_send())
    pl.when(space > 0)(lambda: down().wait_send())

    def arrive(which):
        rows = pl.ds(which * local_bins, local_bins)
        remote(
            edges.at[0], edges_out.at[rows, :], edge_send.at[0], edge_recv.at[which], (space, part)
        ).wait_recv()

    def arrive_all():
        for which in range(bins_count):
            arrive(which)

    pl.when((part == 0) & (space > 0))(arrive_all)
    pl.when((part == bins_count - 1) & (space < space_count - 1))(arrive_all)
    for copy in sends:
        copy.wait()
    for copy in own:
        copy.wait()


def exchange(windows, table, speeds, edges, surface, space_count, bins_count):
    here = pl.BlockSpec(memory_space=pltpu.VMEM)
    local_bins = table.shape[0]
    bins = local_bins * bins_count
    total = space_count * bins_count
    dma = pltpu.SemaphoreType.DMA
    return pl.pallas_call(
        functools.partial(exchange_kernel, space_count, bins_count),
        out_shape=(
            jax.ShapeDtypeStruct((bins, windows.shape[2]), windows.dtype),
            jax.ShapeDtypeStruct((bins, table.shape[1]), table.dtype),
            jax.ShapeDtypeStruct((bins_count,) + speeds.shape, speeds.dtype),
            jax.ShapeDtypeStruct((bins, edges.shape[2]), edges.dtype),
            jax.ShapeDtypeStruct(surface.shape, surface.dtype),
        ),
        in_specs=[here] * 5,
        out_specs=(here,) * 5,
        scratch_shapes=[
            dma((4,)),
            dma((3, bins_count)),
            dma((3, bins_count)),
            dma((2,)),
            dma((bins_count,)),
            dma((total,)),
            dma((total,)),
        ],
        compiler_params=pltpu.CompilerParams(
            collective_id=0, has_side_effects=True, vmem_limit_bytes=32 * 1024 * 1024
        ),
        name="exchange",
    )(windows, table, speeds, edges, surface)


def ocean_kernel(levels, currents_ref, drift_ref, wet_ref, out_ref, drift):
    slots, rows, lanes = currents_ref.shape
    sources, block_rows = drift_ref.shape[0] // slots, drift_ref.shape[1]
    lane = lax.broadcasted_iota(jnp.int32, (rows, lanes), 1)
    level = lax.rem(lane, levels)
    turn = jnp.where(lane < levels, CORIOLIS, -CORIOLIS)
    for slot in range(slots):
        for source in range(sources):
            drift[source * block_rows : (source + 1) * block_rows, :] = drift_ref[
                source * slots + slot
            ].astype(jnp.float32)
        field = currents_ref[slot]
        upper = jnp.where(level == 0, field, pltpu.roll(field, 1, 1))
        lower = jnp.where(level == levels - 1, field, pltpu.roll(field, lanes - 1, 1))
        other = pltpu.roll(field + drift[...], levels, 1)
        moved = field + DT_OCEAN * (turn * other + MIXING * (upper + lower - 2.0 * field))
        wet = jnp.broadcast_to(wet_ref[slot : slot + 1, :].astype(jnp.float32), (lanes, rows)).T
        out_ref[slot] = wet * moved


def ocean_step(currents, drift, wet, levels):
    return pl.pallas_call(
        functools.partial(ocean_kernel, levels),
        out_shape=jax.ShapeDtypeStruct(currents.shape, currents.dtype),
        scratch_shapes=[pltpu.VMEM(currents.shape[1:], jnp.float32)],
        compiler_params=pltpu.CompilerParams(vmem_limit_bytes=16 * 1024 * 1024),
        name="ocean_step",
    )(currents, drift, wet)


def advect_block(energy, speeds, cur_x, cur_y, wet, columns):
    cells = energy.shape[0] - 2 * columns
    mid = slice(columns, columns + cells)
    cx = speeds[0:1, :] + cur_x
    from_before = jnp.maximum(cx[:cells], 0.0) * energy[:cells]
    from_after = jnp.minimum(cx[2 * columns :], 0.0) * energy[2 * columns :]
    own = energy[mid]
    cy = speeds[1:2, :] + cur_y[mid]
    plus = jnp.maximum(cy, 0.0) * own
    minus = jnp.minimum(cy, 0.0) * own
    y = lax.rem(lax.broadcasted_iota(jnp.int32, own.shape, 0), columns)
    plus_prev = jnp.where(y == 0, 0.0, pltpu.roll(plus, 1, 0))
    minus_next = jnp.where(y == columns - 1, 0.0, pltpu.roll(minus, cells - 1, 0))
    moved = own - (jnp.abs(cx[mid]) + jnp.abs(cy)) * own
    moved = moved + from_before - from_after + plus_prev - minus_next
    return (wet * moved).astype(jnp.bfloat16)


def wave_kernel(
    columns,
    chunk,
    win_ref,
    edges_ref,
    mask_ref,
    kernel_ref,
    speeds_ref,
    surface_ref,
    wet_ref,
    ids_ref,
    coef_ref,
    out_ref,
    ext,
    cur,
    wet,
    adv,
    total,
):
    step = pl.program_id(0)
    cells, bins = adv.shape
    levels = kernel_ref.shape[1] // 2

    @pl.when(step == 0)
    def _():
        take_edge = mask_ref[...] > 0.0

        def turn(i, carry):
            rows = pl.ds(pl.multiple_of(i * chunk, chunk), chunk)
            near = win_ref[rows, : 2 * columns].astype(jnp.float32)
            near = jnp.where(take_edge, edges_ref[rows, :].astype(jnp.float32), near).T
            main = win_ref[rows, 2 * columns :].astype(jnp.float32).T
            ext[:columns, rows] = near[:columns].astype(jnp.bfloat16)
            ext[columns : columns + cells, rows] = main.astype(jnp.bfloat16)
            ext[columns + cells :, rows] = near[columns:].astype(jnp.bfloat16)
            return carry

        lax.fori_loop(0, bins // chunk, turn, 0)
        drift = jnp.dot(ext[...], kernel_ref[...], preferred_element_type=jnp.float32)
        half = DT_OCEAN * CORIOLIS

        def wide(row):
            return jnp.broadcast_to(row, (chunk, row.shape[1])).T

        weight = half * wide(surface_ref[2:3, :])
        cur[0] = CURRENT_SCALE * jnp.tanh(
            wide(surface_ref[0:1, :]) + weight * drift[:, levels : levels + 1]
        )
        cur[1] = CURRENT_SCALE * jnp.tanh(
            wide(surface_ref[1:2, :]) - weight * drift[:, 0:1]
        )
        wet[...] = wide(wet_ref[...])

        def one(i, carry):
            lanes = pl.ds(pl.multiple_of(i * chunk, chunk), chunk)
            adv[:, lanes] = advect_block(
                ext[:, lanes].astype(jnp.float32),
                speeds_ref[:, lanes],
                cur[0],
                cur[1],
                wet[...],
                columns,
            )
            return carry

        lax.fori_loop(0, bins // chunk, one, 0)
        total[...] = jnp.zeros_like(total)

    block = ids_ref.shape[1]
    bin_ids = lax.broadcasted_iota(jnp.int32, (bins, block), 0)

    def onehot(which):
        return jnp.where(bin_ids == ids_ref[which : which + 1, :], 1.0, 0.0).astype(jnp.bfloat16)

    first = jnp.dot(adv[...], onehot(0), preferred_element_type=jnp.float32)
    second = jnp.dot(adv[...], onehot(1), preferred_element_type=jnp.float32)
    products = (coef_ref[...] * first * second).astype(jnp.bfloat16)
    total[...] += lax.dot_general(
        products, onehot(2), (((1,), (1,)), ((), ())), preferred_element_type=jnp.float32
    )

    @pl.when(step == pl.num_programs(0) - 1)
    def _():
        out_ref[...] = (adv[...].astype(jnp.float32) + DT_SOURCE * total[...]).astype(jnp.bfloat16)


def wave_step(win, edges, mask, kernel_all, speeds, surface, wet, pair_bins, pair_coef, columns):
    bins, wide = win.shape
    cells = wide - 2 * columns
    pairs = pair_bins.shape[1]
    block = 512 if pairs % 512 == 0 else pairs
    chunk = 128 if bins % 128 == 0 else bins
    whole = lambda shape: pl.BlockSpec(shape, lambda i: (0, 0))
    return pl.pallas_call(
        functools.partial(wave_kernel, columns, chunk),
        grid=(pairs // block,),
        out_shape=jax.ShapeDtypeStruct((cells, bins), jnp.bfloat16),
        in_specs=[
            whole(win.shape),
            whole(edges.shape),
            whole(mask.shape),
            whole(kernel_all.shape),
            whole(speeds.shape),
            whole(surface.shape),
            whole(wet.shape),
            pl.BlockSpec((3, block), lambda i: (0, i)),
            pl.BlockSpec((1, block), lambda i: (0, i)),
        ],
        out_specs=whole((cells, bins)),
        scratch_shapes=[
            pltpu.VMEM((wide, bins), jnp.bfloat16),
            pltpu.VMEM((2, wide, chunk), jnp.float32),
            pltpu.VMEM((cells, chunk), jnp.float32),
            pltpu.VMEM((cells, bins), jnp.bfloat16),
            pltpu.VMEM((cells, bins), jnp.float32),
        ],
        compiler_params=pltpu.CompilerParams(vmem_limit_bytes=48 * 1024 * 1024),
        cost_estimate=pl.CostEstimate(
            flops=6 * pairs * bins * cells, bytes_accessed=4 * bins * wide, transcendentals=0
        ),
        name="wave_step",
    )(win, edges, mask, kernel_all, speeds, surface, wet, pair_bins, pair_coef[None, :])


def per_device(
    spectrum,
    group_speed,
    stokes_kernel,
    pair_bins,
    pair_coef,
    currents,
    col_map,
    wave_wet,
    ocean_wet,
):
    local_bins, tile_rows, columns = spectrum.shape
    space_count = lax.axis_size("space")
    bins_count = lax.axis_size("bins")
    groups = space_count * bins_count
    group_cols = columns // groups
    levels = stokes_kernel.shape[1] // 2
    block_rows = tile_rows // bins_count
    width = block_rows * columns
    slot_col = (
        col_map[:, None] * group_cols + jnp.arange(group_cols, dtype=jnp.int32)[None, :]
    ).reshape(-1)

    wet_f = ocean_wet.astype(jnp.float32)
    u0, u1 = currents[:, :, 0], currents[:, :, 1]
    v0, v1 = currents[:, :, levels], currents[:, :, levels + 1]
    su = wet_f * (u0 + DT_OCEAN * (CORIOLIS * v0 + MIXING * (u1 - u0)))
    sv = wet_f * (v0 + DT_OCEAN * (-CORIOLIS * u0 + MIXING * (v1 - v0)))
    surface = jnp.stack([su, sv, wet_f])

    def windows_of(rows, before, after):
        before = jnp.concatenate([before, rows[..., :-1, -1:]], axis=-2)
        after = jnp.concatenate([rows[..., 1:, :1], after], axis=-2)
        return jnp.concatenate([before, after, rows], axis=-1)

    none = jnp.zeros((3, group_cols, 1, 1), jnp.float32)
    surface = windows_of(
        surface.reshape(3, group_cols, groups, block_rows), none, none
    )
    window_rows = block_rows + 2
    surface = jnp.transpose(surface, (2, 0, 1, 3)).reshape(groups, 1, 3 * group_cols * window_rows)
    used = surface.shape[2]
    surface = jnp.pad(surface, ((0, 0), (0, 0), (0, -used % 128)))

    rows = spectrum.reshape(local_bins, bins_count, width)
    zeros = jnp.zeros((local_bins, 1, columns), spectrum.dtype)
    before = jnp.concatenate([zeros, rows[:, :-1, width - columns :]], axis=1)
    after = jnp.concatenate([rows[:, 1:, :columns], zeros], axis=1)
    windows = jnp.transpose(jnp.concatenate([before, after, rows], axis=2), (1, 0, 2))
    zero = zeros[:, 0]
    edges = jnp.stack(
        [
            jnp.concatenate([spectrum[:, -1, :], zero], axis=1),
            jnp.concatenate([zero, spectrum[:, 0, :]], axis=1),
        ]
    )
    speeds = jnp.pad(group_speed, ((0, -2 % 8), (0, -local_bins % 128)))
    win, kernel_all, speeds, edges, surface = exchange(
        windows, stokes_kernel, speeds, edges, surface, space_count, bins_count
    )
    speeds = jnp.transpose(speeds[:, :2, :local_bins], (1, 0, 2)).reshape(2, -1)
    space, part = lax.axis_index("space"), lax.axis_index("bins")
    from_below = (part == 0) & (space > 0)
    from_above = (part == bins_count - 1) & (space < space_count - 1)
    is_below = jnp.arange(2 * columns, dtype=jnp.int32) < columns
    take_edge = jnp.where(is_below, from_below, from_above)
    take_edge = take_edge.astype(jnp.float32)[None, :]
    drift_main = lax.dot_general(
        win[:, 2 * columns :],
        kernel_all,
        (((0,), (0,)), ((), ())),
        preferred_element_type=jnp.float32,
    )
    mine = surface[:, 0, :used].reshape(groups, 3, group_cols, window_rows)
    mine = jnp.transpose(mine, (0, 2, 1, 3)).reshape(groups * group_cols, 3, window_rows)
    here = slot_col[:, None] == jnp.arange(columns, dtype=jnp.int32)[None, :]
    mine = jnp.sum(jnp.where(here[:, None, None, :], mine[:, :, :, None], 0.0), axis=0)
    mine = jnp.concatenate([mine[:, :1], mine[:, 2:], mine[:, 1:2]], axis=1)
    mine = mine.reshape(3, window_rows * columns)
    wet_rows = lax.dynamic_slice_in_dim(
        wave_wet, lax.axis_index("bins") * block_rows, block_rows, 0
    )
    wet_rows = wet_rows.astype(jnp.float32).reshape(1, width)

    inner = drift_main.reshape(block_rows, columns, 2 * levels)
    routed = jnp.einsum(
        "jc,xcl->jxl",
        here.astype(jnp.bfloat16),
        inner.astype(jnp.bfloat16),
        preferred_element_type=jnp.float32,
    ).astype(jnp.bfloat16)
    drift = lax.all_to_all(
        routed, ("space", "bins"), split_axis=0, concat_axis=0, tiled=True
    )
    new_currents = ocean_step(currents, drift, ocean_wet, levels)

    updated = wave_step(
        win, edges, take_edge, kernel_all, speeds, mine, wet_rows, pair_bins, pair_coef, columns
    )
    new_spectrum = jnp.transpose(
        updated.reshape(block_rows, columns, bins_count * local_bins), (2, 0, 1)
    )
    return (new_spectrum, new_currents)


def solution(mesh):
    placed = (
        P("bins", "space", None),
        P(None, "bins"),
        P("bins", None),
        P(),
        P(),
        P(("space", "bins"), None, None),
        P(),
        P("space", None),
        P(("space", "bins"), None),
    )
    return jax.shard_map(
        per_device,
        mesh=mesh,
        in_specs=placed,
        out_specs=(P(None, ("space", "bins"), None), P(("space", "bins"), None, None)),
        check_vma=False,
    )
```

```python
import functools
import jax
import jax.numpy as jnp
from jax import lax
from jax.experimental import pallas as pl
from jax.experimental.pallas import tpu as pltpu
from jax.sharding import PartitionSpec as P

DT_OCEAN = 0.5
CORIOLIS = 0.8
MIXING = 0.4
CURRENT_SCALE = 0.15
DT_SOURCE = 0.5


def surface_kernel(levels, block_rows, currents_ref, wet_ref, out_ref, held):
    slots, rows, lanes = currents_ref.shape
    groups = rows // block_rows
    held[...] = jnp.zeros_like(held)
    for slot in range(slots):
        wet = jnp.broadcast_to(wet_ref[slot : slot + 1, :].astype(jnp.float32), (lanes, rows)).T
        field = currents_ref[slot]
        below = pltpu.roll(field, lanes - 1, 1)
        other = pltpu.roll(field, levels, 1)
        lane = lax.broadcasted_iota(jnp.int32, (rows, lanes), 1)
        turn = jnp.where(lane < levels, CORIOLIS, -CORIOLIS)
        moved = wet * (field + DT_OCEAN * (turn * other + MIXING * (below - field)))
        inner = pl.ds(8, rows)
        held[inner, slot : slot + 1] = moved[:, 0:1]
        held[inner, slots + slot : slots + slot + 1] = moved[:, levels : levels + 1]
        held[inner, 2 * slots + slot : 2 * slots + slot + 1] = wet[:, 0:1]
    sent = jnp.zeros((groups, lanes), jnp.float32)
    for row in range(block_rows + 2):
        part = held[pl.ds(7 + row, groups, stride=block_rows), :]
        sent = sent + (pltpu.roll(part, 8 * row, 1) if row else part)
    out_ref[...] = sent


def surface_windows(currents, wet, levels, block_rows):
    rows, lanes = currents.shape[1:]
    return pl.pallas_call(
        functools.partial(surface_kernel, levels, block_rows),
        out_shape=jax.ShapeDtypeStruct((rows // block_rows, lanes), jnp.float32),
        scratch_shapes=[pltpu.VMEM((rows + 16, lanes), jnp.float32)],
        compiler_params=pltpu.CompilerParams(vmem_limit_bytes=16 * 1024 * 1024),
        name="surface_windows",
    )(currents, wet)


def exchange_kernel(
    space_count,
    bins_count,
    windows,
    table,
    speeds,
    edges,
    surface,
    windows_out,
    table_out,
    speeds_out,
    edges_out,
    surface_out,
    own_sem,
    send_sem,
    recv_sem,
    edge_send,
    edge_recv,
    surface_send,
    surface_recv,
):
    space, part = lax.axis_index("space"), lax.axis_index("bins")
    total = space_count * bins_count
    me = space * bins_count + part
    local_bins = table.shape[0]
    mine = pl.ds(pl.multiple_of(part * local_bins, 32), local_bins)

    def place(other):
        return (other // bins_count, lax.rem(other, bins_count))

    def remote(source, target, sent, received, device):
        return pltpu.make_async_remote_copy(
            src_ref=source,
            dst_ref=target,
            send_sem=sent,
            recv_sem=received,
            device_id=device,
            device_id_type=pl.DeviceIdType.MESH,
        )

    own = [
        pltpu.make_async_copy(windows.at[part], windows_out.at[mine, :], own_sem.at[0]),
        pltpu.make_async_copy(table, table_out.at[mine, :], own_sem.at[1]),
        pltpu.make_async_copy(speeds, speeds_out.at[part], own_sem.at[2]),
        pltpu.make_async_copy(surface.at[me], surface_out.at[me], own_sem.at[3]),
    ]
    for copy in own:
        copy.start()

    barrier = pltpu.get_barrier_semaphore()

    def greet(k, carry):
        pl.semaphore_signal(
            barrier,
            inc=1,
            device_id=place(lax.rem(me + k, total)),
            device_id_type=pl.DeviceIdType.MESH,
        )
        return carry

    lax.fori_loop(1, total, greet, 0)
    pl.semaphore_wait(barrier, total - 1)

    sends = []
    for j in range(1, bins_count):
        peer = lax.rem(part + j, bins_count)
        device = (space, peer)
        sends.append(
            remote(speeds, speeds_out.at[part], send_sem.at[0, j], recv_sem.at[0, j], device)
        )
        sends.append(
            remote(table, table_out.at[mine, :], send_sem.at[1, j], recv_sem.at[1, j], device)
        )
        sends.append(
            remote(
                windows.at[peer],
                windows_out.at[mine, :],
                send_sem.at[2, j],
                recv_sem.at[2, j],
                device,
            )
        )
    for copy in sends:
        copy.start()

    def up():
        return remote(
            edges.at[0],
            edges_out.at[mine, :],
            edge_send.at[0],
            edge_recv.at[part],
            (space + 1, 0),
        )

    def down():
        return remote(
            edges.at[1],
            edges_out.at[mine, :],
            edge_send.at[1],
            edge_recv.at[part],
            (space - 1, bins_count - 1),
        )

    pl.when(space < space_count - 1)(lambda: up().start())
    pl.when(space > 0)(lambda: down().start())

    def to_other(k):
        other = lax.rem(me + k, total)
        return remote(
            surface.at[other],
            surface_out.at[me],
            surface_send.at[k],
            surface_recv.at[k],
            place(other),
        )

    def start_one(k, carry):
        to_other(k).start()
        return carry

    def finish_one(k, carry):
        to_other(k).wait()
        return carry

    lax.fori_loop(1, total, start_one, 0)
    lax.fori_loop(1, total, finish_one, 0)
    pl.when(space < space_count - 1)(lambda: up().wait_send())
    pl.when(space > 0)(lambda: down().wait_send())

    def arrive(which):
        rows = pl.ds(which * local_bins, local_bins)
        remote(
            edges.at[0], edges_out.at[rows, :], edge_send.at[0], edge_recv.at[which], (space, part)
        ).wait_recv()

    def arrive_all():
        for which in range(bins_count):
            arrive(which)

    pl.when((part == 0) & (space > 0))(arrive_all)
    pl.when((part == bins_count - 1) & (space < space_count - 1))(arrive_all)
    for copy in sends:
        copy.wait()
    for copy in own:
        copy.wait()


def exchange(windows, table, speeds, edges, surface, space_count, bins_count):
    here = pl.BlockSpec(memory_space=pltpu.VMEM)
    local_bins = table.shape[0]
    bins = local_bins * bins_count
    total = space_count * bins_count
    dma = pltpu.SemaphoreType.DMA
    return pl.pallas_call(
        functools.partial(exchange_kernel, space_count, bins_count),
        out_shape=(
            jax.ShapeDtypeStruct((bins, windows.shape[2]), windows.dtype),
            jax.ShapeDtypeStruct((bins, table.shape[1]), table.dtype),
            jax.ShapeDtypeStruct((bins_count,) + speeds.shape, speeds.dtype),
            jax.ShapeDtypeStruct((bins, edges.shape[2]), edges.dtype),
            jax.ShapeDtypeStruct(surface.shape, surface.dtype),
        ),
        in_specs=[here] * 5,
        out_specs=(here,) * 5,
        scratch_shapes=[
            dma((4,)),
            dma((3, bins_count)),
            dma((3, bins_count)),
            dma((2,)),
            dma((bins_count,)),
            dma((total,)),
            dma((total,)),
        ],
        compiler_params=pltpu.CompilerParams(
            collective_id=0, has_side_effects=True, vmem_limit_bytes=32 * 1024 * 1024
        ),
        name="exchange",
    )(windows, table, speeds, edges, surface)


def ocean_kernel(levels, currents_ref, drift_ref, wet_ref, out_ref, drift):
    slots, rows, lanes = currents_ref.shape
    sources, block_rows = drift_ref.shape[0] // slots, drift_ref.shape[1]
    lane = lax.broadcasted_iota(jnp.int32, (rows, lanes), 1)
    level = lax.rem(lane, levels)
    turn = jnp.where(lane < levels, CORIOLIS, -CORIOLIS)
    for slot in range(slots):
        for source in range(sources):
            drift[source * block_rows : (source + 1) * block_rows, :] = drift_ref[
                source * slots + slot
            ].astype(jnp.float32)
        field = currents_ref[slot]
        upper = jnp.where(level == 0, field, pltpu.roll(field, 1, 1))
        lower = jnp.where(level == levels - 1, field, pltpu.roll(field, lanes - 1, 1))
        other = pltpu.roll(field + drift[...], levels, 1)
        moved = field + DT_OCEAN * (turn * other + MIXING * (upper + lower - 2.0 * field))
        wet = jnp.broadcast_to(wet_ref[slot : slot + 1, :].astype(jnp.float32), (lanes, rows)).T
        out_ref[slot] = wet * moved


def ocean_step(currents, drift, wet, levels):
    return pl.pallas_call(
        functools.partial(ocean_kernel, levels),
        out_shape=jax.ShapeDtypeStruct(currents.shape, currents.dtype),
        scratch_shapes=[pltpu.VMEM(currents.shape[1:], jnp.float32)],
        compiler_params=pltpu.CompilerParams(vmem_limit_bytes=16 * 1024 * 1024),
        name="ocean_step",
    )(currents, drift, wet)


def advect_block(energy, speeds, cur_x, cur_y, wet, columns):
    cells = energy.shape[0] - 2 * columns
    mid = slice(columns, columns + cells)
    cx = speeds[0:1, :] + cur_x
    from_before = jnp.maximum(cx[:cells], 0.0) * energy[:cells]
    from_after = jnp.minimum(cx[2 * columns :], 0.0) * energy[2 * columns :]
    own = energy[mid]
    cy = speeds[1:2, :] + cur_y[mid]
    plus = jnp.maximum(cy, 0.0) * own
    minus = jnp.minimum(cy, 0.0) * own
    y = lax.rem(lax.broadcasted_iota(jnp.int32, own.shape, 0), columns)
    plus_prev = jnp.where(y == 0, 0.0, pltpu.roll(plus, 1, 0))
    minus_next = jnp.where(y == columns - 1, 0.0, pltpu.roll(minus, cells - 1, 0))
    moved = own - (jnp.abs(cx[mid]) + jnp.abs(cy)) * own
    moved = moved + from_before - from_after + plus_prev - minus_next
    return (wet * moved).astype(jnp.bfloat16)


def wave_kernel(
    columns,
    chunk,
    win_ref,
    edges_ref,
    mask_ref,
    kernel_ref,
    speeds_ref,
    surface_ref,
    wet_ref,
    ids_ref,
    coef_ref,
    out_ref,
    ext,
    cur,
    wet,
    adv,
    total,
):
    step = pl.program_id(0)
    cells, bins = adv.shape
    levels = kernel_ref.shape[1] // 2

    @pl.when(step == 0)
    def _():
        take_edge = mask_ref[...] > 0.0

        def turn(i, carry):
            rows = pl.ds(pl.multiple_of(i * chunk, chunk), chunk)
            near = win_ref[rows, : 2 * columns].astype(jnp.float32)
            near = jnp.where(take_edge, edges_ref[rows, :].astype(jnp.float32), near).T
            main = win_ref[rows, 2 * columns :].astype(jnp.float32).T
            ext[:columns, rows] = near[:columns].astype(jnp.bfloat16)
            ext[columns : columns + cells, rows] = main.astype(jnp.bfloat16)
            ext[columns + cells :, rows] = near[columns:].astype(jnp.bfloat16)
            return carry

        lax.fori_loop(0, bins // chunk, turn, 0)
        drift = jnp.dot(ext[...], kernel_ref[...], preferred_element_type=jnp.float32)
        half = DT_OCEAN * CORIOLIS

        def wide(row):
            return jnp.broadcast_to(row, (chunk, row.shape[1])).T

        weight = half * wide(surface_ref[2:3, :])
        cur[0] = CURRENT_SCALE * jnp.tanh(
            wide(surface_ref[0:1, :]) + weight * drift[:, levels : levels + 1]
        )
        cur[1] = CURRENT_SCALE * jnp.tanh(
            wide(surface_ref[1:2, :]) - weight * drift[:, 0:1]
        )
        wet[...] = wide(wet_ref[...])

        def one(i, carry):
            lanes = pl.ds(pl.multiple_of(i * chunk, chunk), chunk)
            adv[:, lanes] = advect_block(
                ext[:, lanes].astype(jnp.float32),
                speeds_ref[:, lanes],
                cur[0],
                cur[1],
                wet[...],
                columns,
            )
            return carry

        lax.fori_loop(0, bins // chunk, one, 0)
        total[...] = jnp.zeros_like(total)

    block = ids_ref.shape[1]
    bin_ids = lax.broadcasted_iota(jnp.int32, (bins, block), 0)

    def onehot(which):
        return jnp.where(bin_ids == ids_ref[which : which + 1, :], 1.0, 0.0).astype(jnp.bfloat16)

    first = jnp.dot(adv[...], onehot(0), preferred_element_type=jnp.float32)
    second = jnp.dot(adv[...], onehot(1), preferred_element_type=jnp.float32)
    products = (coef_ref[...] * first * second).astype(jnp.bfloat16)
    total[...] += lax.dot_general(
        products, onehot(2), (((1,), (1,)), ((), ())), preferred_element_type=jnp.float32
    )

    @pl.when(step == pl.num_programs(0) - 1)
    def _():
        out_ref[...] = (adv[...].astype(jnp.float32) + DT_SOURCE * total[...]).astype(jnp.bfloat16)


def wave_step(win, edges, mask, kernel_all, speeds, surface, wet, pair_bins, pair_coef, columns):
    bins, wide = win.shape
    cells = wide - 2 * columns
    pairs = pair_bins.shape[1]
    block = 512 if pairs % 512 == 0 else pairs
    chunk = 128 if bins % 128 == 0 else bins
    whole = lambda shape: pl.BlockSpec(shape, lambda i: (0, 0))
    return pl.pallas_call(
        functools.partial(wave_kernel, columns, chunk),
        grid=(pairs // block,),
        out_shape=jax.ShapeDtypeStruct((cells, bins), jnp.bfloat16),
        in_specs=[
            whole(win.shape),
            whole(edges.shape),
            whole(mask.shape),
            whole(kernel_all.shape),
            whole(speeds.shape),
            whole(surface.shape),
            whole(wet.shape),
            pl.BlockSpec((3, block), lambda i: (0, i)),
            pl.BlockSpec((1, block), lambda i: (0, i)),
        ],
        out_specs=whole((cells, bins)),
        scratch_shapes=[
            pltpu.VMEM((wide, bins), jnp.bfloat16),
            pltpu.VMEM((2, wide, chunk), jnp.float32),
            pltpu.VMEM((cells, chunk), jnp.float32),
            pltpu.VMEM((cells, bins), jnp.bfloat16),
            pltpu.VMEM((cells, bins), jnp.float32),
        ],
        compiler_params=pltpu.CompilerParams(vmem_limit_bytes=48 * 1024 * 1024),
        cost_estimate=pl.CostEstimate(
            flops=6 * pairs * bins * cells, bytes_accessed=4 * bins * wide, transcendentals=0
        ),
        name="wave_step",
    )(win, edges, mask, kernel_all, speeds, surface, wet, pair_bins, pair_coef[None, :])


def per_device(
    spectrum,
    group_speed,
    stokes_kernel,
    pair_bins,
    pair_coef,
    currents,
    col_map,
    wave_wet,
    ocean_wet,
):
    local_bins, tile_rows, columns = spectrum.shape
    space_count = lax.axis_size("space")
    bins_count = lax.axis_size("bins")
    groups = space_count * bins_count
    group_cols = columns // groups
    levels = stokes_kernel.shape[1] // 2
    block_rows = tile_rows // bins_count
    width = block_rows * columns
    slot_col = (
        col_map[:, None] * group_cols + jnp.arange(group_cols, dtype=jnp.int32)[None, :]
    ).reshape(-1)

    window_rows = block_rows + 2
    surface = surface_windows(currents, ocean_wet, levels, block_rows)[:, None, :]

    rows = spectrum.reshape(local_bins, bins_count, width)
    zeros = jnp.zeros((local_bins, 1, columns), spectrum.dtype)
    before = jnp.concatenate([zeros, rows[:, :-1, width - columns :]], axis=1)
    after = jnp.concatenate([rows[:, 1:, :columns], zeros], axis=1)
    windows = jnp.transpose(jnp.concatenate([before, after, rows], axis=2), (1, 0, 2))
    zero = zeros[:, 0]
    edges = jnp.stack(
        [
            jnp.concatenate([spectrum[:, -1, :], zero], axis=1),
            jnp.concatenate([zero, spectrum[:, 0, :]], axis=1),
        ]
    )
    speeds = jnp.pad(group_speed, ((0, -2 % 8), (0, -local_bins % 128)))
    win, kernel_all, speeds, edges, surface = exchange(
        windows, stokes_kernel, speeds, edges, surface, space_count, bins_count
    )
    speeds = jnp.transpose(speeds[:, :2, :local_bins], (1, 0, 2)).reshape(2, -1)
    space, part = lax.axis_index("space"), lax.axis_index("bins")
    from_below = (part == 0) & (space > 0)
    from_above = (part == bins_count - 1) & (space < space_count - 1)
    is_below = jnp.arange(2 * columns, dtype=jnp.int32) < columns
    take_edge = jnp.where(is_below, from_below, from_above)
    take_edge = take_edge.astype(jnp.float32)[None, :]
    drift_main = lax.dot_general(
        win[:, 2 * columns :],
        kernel_all,
        (((0,), (0,)), ((), ())),
        preferred_element_type=jnp.float32,
    )
    mine = surface[:, 0, : 8 * window_rows].reshape(groups, window_rows, 8)
    mine = mine[:, :, : 3 * group_cols].reshape(groups, window_rows, 3, group_cols)
    mine = jnp.transpose(mine, (0, 3, 2, 1)).reshape(groups * group_cols, 3, window_rows)
    here = slot_col[:, None] == jnp.arange(columns, dtype=jnp.int32)[None, :]
    mine = jnp.sum(jnp.where(here[:, None, None, :], mine[:, :, :, None], 0.0), axis=0)
    mine = mine.reshape(3, window_rows * columns)
    wet_rows = wave_wet.astype(jnp.float32).reshape(bins_count, block_rows, columns)
    is_mine = jnp.arange(bins_count, dtype=jnp.int32) == part
    wet_rows = jnp.sum(jnp.where(is_mine[:, None, None], wet_rows, 0.0), axis=0).reshape(1, width)

    inner = drift_main.reshape(block_rows, columns, 2 * levels)
    routed = jnp.einsum(
        "jc,xcl->jxl",
        here.astype(jnp.bfloat16),
        inner.astype(jnp.bfloat16),
        preferred_element_type=jnp.float32,
    ).astype(jnp.bfloat16)
    drift = lax.all_to_all(
        routed, ("space", "bins"), split_axis=0, concat_axis=0, tiled=True
    )
    new_currents = ocean_step(currents, drift, ocean_wet, levels)

    updated = wave_step(
        win, edges, take_edge, kernel_all, speeds, mine, wet_rows, pair_bins, pair_coef, columns
    )
    new_spectrum = jnp.transpose(
        updated.reshape(block_rows, columns, bins_count * local_bins), (2, 0, 1)
    )
    return (new_spectrum, new_currents)


def solution(mesh):
    placed = (
        P("bins", "space", None),
        P(None, "bins"),
        P("bins", None),
        P(),
        P(),
        P(("space", "bins"), None, None),
        P(),
        P("space", None),
        P(("space", "bins"), None),
    )
    return jax.shard_map(
        per_device,
        mesh=mesh,
        in_specs=placed,
        out_specs=(P(None, ("space", "bins"), None), P(("space", "bins"), None, None)),
        check_vma=False,
    )
```

```python
import functools
import jax
import jax.numpy as jnp
from jax import lax
from jax.experimental import pallas as pl
from jax.experimental.pallas import tpu as pltpu
from jax.sharding import PartitionSpec as P

DT_OCEAN = 0.5
CORIOLIS = 0.8
MIXING = 0.4
CURRENT_SCALE = 0.15
DT_SOURCE = 0.5


def surface_kernel(levels, block_rows, currents_ref, wet_ref, out_ref, held):
    slots, rows, lanes = currents_ref.shape
    groups = rows // block_rows
    held[...] = jnp.zeros_like(held)
    for slot in range(slots):
        wet = jnp.broadcast_to(wet_ref[slot : slot + 1, :].astype(jnp.float32), (lanes, rows)).T
        field = currents_ref[slot]
        below = pltpu.roll(field, lanes - 1, 1)
        other = pltpu.roll(field, levels, 1)
        lane = lax.broadcasted_iota(jnp.int32, (rows, lanes), 1)
        turn = jnp.where(lane < levels, CORIOLIS, -CORIOLIS)
        moved = wet * (field + DT_OCEAN * (turn * other + MIXING * (below - field)))
        inner = pl.ds(8, rows)
        held[inner, slot : slot + 1] = moved[:, 0:1]
        held[inner, slots + slot : slots + slot + 1] = moved[:, levels : levels + 1]
        held[inner, 2 * slots + slot : 2 * slots + slot + 1] = wet[:, 0:1]
    sent = jnp.zeros((groups, lanes), jnp.float32)
    for row in range(block_rows + 2):
        part = held[pl.ds(7 + row, groups, stride=block_rows), :]
        sent = sent + (pltpu.roll(part, 8 * row, 1) if row else part)
    out_ref[...] = sent


def surface_windows(currents, wet, levels, block_rows):
    rows, lanes = currents.shape[1:]
    return pl.pallas_call(
        functools.partial(surface_kernel, levels, block_rows),
        out_shape=jax.ShapeDtypeStruct((rows // block_rows, lanes), jnp.float32),
        scratch_shapes=[pltpu.VMEM((rows + 16, lanes), jnp.float32)],
        compiler_params=pltpu.CompilerParams(vmem_limit_bytes=16 * 1024 * 1024),
        name="surface_windows",
    )(currents, wet)


def exchange_kernel(
    space_count,
    bins_count,
    windows,
    table,
    speeds,
    edges,
    surface,
    windows_out,
    table_out,
    speeds_out,
    edges_out,
    surface_out,
    own_sem,
    send_sem,
    recv_sem,
    edge_send,
    edge_recv,
    surface_send,
    surface_recv,
):
    space, part = lax.axis_index("space"), lax.axis_index("bins")
    total = space_count * bins_count
    me = space * bins_count + part
    local_bins = table.shape[0]
    mine = pl.ds(pl.multiple_of(part * local_bins, 32), local_bins)

    def place(other):
        return (other // bins_count, lax.rem(other, bins_count))

    def remote(source, target, sent, received, device):
        return pltpu.make_async_remote_copy(
            src_ref=source,
            dst_ref=target,
            send_sem=sent,
            recv_sem=received,
            device_id=device,
            device_id_type=pl.DeviceIdType.MESH,
        )

    own = [
        pltpu.make_async_copy(windows.at[part], windows_out.at[mine, :], own_sem.at[0]),
        pltpu.make_async_copy(table, table_out.at[mine, :], own_sem.at[1]),
        pltpu.make_async_copy(speeds, speeds_out.at[part], own_sem.at[2]),
        pltpu.make_async_copy(surface.at[me], surface_out.at[me], own_sem.at[3]),
    ]
    barrier = pltpu.get_barrier_semaphore()

    def greet(k, carry):
        pl.semaphore_signal(
            barrier,
            inc=1,
            device_id=place(lax.rem(me + k, total)),
            device_id_type=pl.DeviceIdType.MESH,
        )
        return carry

    lax.fori_loop(1, total, greet, 0)
    pl.semaphore_wait(barrier, total - 1)

    sends = []
    for j in sorted(range(1, bins_count), key=lambda j: abs(2 * j - bins_count)):
        peer = lax.rem(part + j, bins_count)
        device = (space, peer)
        sends.append(
            remote(speeds, speeds_out.at[part], send_sem.at[0, j], recv_sem.at[0, j], device)
        )
        sends.append(
            remote(table, table_out.at[mine, :], send_sem.at[1, j], recv_sem.at[1, j], device)
        )
        sends.append(
            remote(
                windows.at[peer],
                windows_out.at[mine, :],
                send_sem.at[2, j],
                recv_sem.at[2, j],
                device,
            )
        )
    for copy in sends[2::3] + sends[1::3] + sends[0::3]:
        copy.start()
    for copy in own:
        copy.start()

    def up():
        return remote(
            edges.at[0],
            edges_out.at[mine, :],
            edge_send.at[0],
            edge_recv.at[part],
            (space + 1, 0),
        )

    def down():
        return remote(
            edges.at[1],
            edges_out.at[mine, :],
            edge_send.at[1],
            edge_recv.at[part],
            (space - 1, bins_count - 1),
        )

    pl.when(space < space_count - 1)(lambda: up().start())
    pl.when(space > 0)(lambda: down().start())

    def to_other(k):
        other = lax.rem(me + k, total)
        return remote(
            surface.at[other],
            surface_out.at[me],
            surface_send.at[k],
            surface_recv.at[k],
            place(other),
        )

    def start_one(k, carry):
        to_other(k).start()
        return carry

    def finish_one(k, carry):
        to_other(k).wait()
        return carry

    lax.fori_loop(1, total, start_one, 0)
    lax.fori_loop(1, total, finish_one, 0)
    pl.when(space < space_count - 1)(lambda: up().wait_send())
    pl.when(space > 0)(lambda: down().wait_send())

    def arrive(which):
        rows = pl.ds(which * local_bins, local_bins)
        remote(
            edges.at[0], edges_out.at[rows, :], edge_send.at[0], edge_recv.at[which], (space, part)
        ).wait_recv()

    def arrive_all():
        for which in range(bins_count):
            arrive(which)

    pl.when((part == 0) & (space > 0))(arrive_all)
    pl.when((part == bins_count - 1) & (space < space_count - 1))(arrive_all)
    for copy in sends:
        copy.wait()
    for copy in own:
        copy.wait()


def exchange(windows, table, speeds, edges, surface, space_count, bins_count):
    here = pl.BlockSpec(memory_space=pltpu.VMEM)
    local_bins = table.shape[0]
    bins = local_bins * bins_count
    total = space_count * bins_count
    dma = pltpu.SemaphoreType.DMA
    return pl.pallas_call(
        functools.partial(exchange_kernel, space_count, bins_count),
        out_shape=(
            jax.ShapeDtypeStruct((bins, windows.shape[2]), windows.dtype),
            jax.ShapeDtypeStruct((bins, table.shape[1]), table.dtype),
            jax.ShapeDtypeStruct((bins_count,) + speeds.shape, speeds.dtype),
            jax.ShapeDtypeStruct((bins, edges.shape[2]), edges.dtype),
            jax.ShapeDtypeStruct(surface.shape, surface.dtype),
        ),
        in_specs=[here] * 5,
        out_specs=(here,) * 5,
        scratch_shapes=[
            dma((4,)),
            dma((3, bins_count)),
            dma((3, bins_count)),
            dma((2,)),
            dma((bins_count,)),
            dma((total,)),
            dma((total,)),
        ],
        compiler_params=pltpu.CompilerParams(
            collective_id=0, has_side_effects=True, vmem_limit_bytes=32 * 1024 * 1024
        ),
        name="exchange",
    )(windows, table, speeds, edges, surface)


def ocean_kernel(levels, currents_ref, drift_ref, wet_ref, out_ref, drift):
    slots, rows, lanes = currents_ref.shape
    sources, block_rows = drift_ref.shape[0] // slots, drift_ref.shape[1]
    lane = lax.broadcasted_iota(jnp.int32, (rows, lanes), 1)
    level = lax.rem(lane, levels)
    turn = jnp.where(lane < levels, CORIOLIS, -CORIOLIS)
    for slot in range(slots):
        for source in range(sources):
            drift[source * block_rows : (source + 1) * block_rows, :] = drift_ref[
                source * slots + slot
            ].astype(jnp.float32)
        field = currents_ref[slot]
        upper = jnp.where(level == 0, field, pltpu.roll(field, 1, 1))
        lower = jnp.where(level == levels - 1, field, pltpu.roll(field, lanes - 1, 1))
        other = pltpu.roll(field + drift[...], levels, 1)
        moved = field + DT_OCEAN * (turn * other + MIXING * (upper + lower - 2.0 * field))
        wet = jnp.broadcast_to(wet_ref[slot : slot + 1, :].astype(jnp.float32), (lanes, rows)).T
        out_ref[slot] = wet * moved


def ocean_step(currents, drift, wet, levels):
    return pl.pallas_call(
        functools.partial(ocean_kernel, levels),
        out_shape=jax.ShapeDtypeStruct(currents.shape, currents.dtype),
        scratch_shapes=[pltpu.VMEM(currents.shape[1:], jnp.float32)],
        compiler_params=pltpu.CompilerParams(vmem_limit_bytes=16 * 1024 * 1024),
        name="ocean_step",
    )(currents, drift, wet)


def advect_block(energy, speeds, cur_x, cur_y, wet, columns):
    cells = energy.shape[0] - 2 * columns
    mid = slice(columns, columns + cells)
    cx = speeds[0:1, :] + cur_x
    from_before = jnp.maximum(cx[:cells], 0.0) * energy[:cells]
    from_after = jnp.minimum(cx[2 * columns :], 0.0) * energy[2 * columns :]
    own = energy[mid]
    cy = speeds[1:2, :] + cur_y[mid]
    plus = jnp.maximum(cy, 0.0) * own
    minus = jnp.minimum(cy, 0.0) * own
    y = lax.rem(lax.broadcasted_iota(jnp.int32, own.shape, 0), columns)
    plus_prev = jnp.where(y == 0, 0.0, pltpu.roll(plus, 1, 0))
    minus_next = jnp.where(y == columns - 1, 0.0, pltpu.roll(minus, cells - 1, 0))
    moved = own - (jnp.abs(cx[mid]) + jnp.abs(cy)) * own
    moved = moved + from_before - from_after + plus_prev - minus_next
    return (wet * moved).astype(jnp.bfloat16)


def wave_kernel(
    columns,
    chunk,
    win_ref,
    edges_ref,
    mask_ref,
    kernel_ref,
    speeds_ref,
    surface_ref,
    wet_ref,
    ids_ref,
    coef_ref,
    out_ref,
    ext,
    cur,
    wet,
    adv,
    total,
):
    step = pl.program_id(0)
    cells, bins = adv.shape
    levels = kernel_ref.shape[1] // 2

    @pl.when(step == 0)
    def _():
        take_edge = mask_ref[...] > 0.0

        def turn(i, carry):
            rows = pl.ds(pl.multiple_of(i * chunk, chunk), chunk)
            near = win_ref[rows, : 2 * columns].astype(jnp.float32)
            near = jnp.where(take_edge, edges_ref[rows, :].astype(jnp.float32), near).T
            main = win_ref[rows, 2 * columns :].astype(jnp.float32).T
            ext[:columns, rows] = near[:columns].astype(jnp.bfloat16)
            ext[columns : columns + cells, rows] = main.astype(jnp.bfloat16)
            ext[columns + cells :, rows] = near[columns:].astype(jnp.bfloat16)
            return carry

        lax.fori_loop(0, bins // chunk, turn, 0)
        drift = jnp.dot(ext[...], kernel_ref[...], preferred_element_type=jnp.float32)
        half = DT_OCEAN * CORIOLIS

        def wide(row):
            return jnp.broadcast_to(row, (chunk, row.shape[1])).T

        weight = half * wide(surface_ref[2:3, :])
        cur[0] = CURRENT_SCALE * jnp.tanh(
            wide(surface_ref[0:1, :]) + weight * drift[:, levels : levels + 1]
        )
        cur[1] = CURRENT_SCALE * jnp.tanh(
            wide(surface_ref[1:2, :]) - weight * drift[:, 0:1]
        )
        wet[...] = wide(wet_ref[...])

        def one(i, carry):
            lanes = pl.ds(pl.multiple_of(i * chunk, chunk), chunk)
            adv[:, lanes] = advect_block(
                ext[:, lanes].astype(jnp.float32),
                speeds_ref[:, lanes],
                cur[0],
                cur[1],
                wet[...],
                columns,
            )
            return carry

        lax.fori_loop(0, bins // chunk, one, 0)
        total[...] = jnp.zeros_like(total)

    block = ids_ref.shape[1]
    bin_ids = lax.broadcasted_iota(jnp.int32, (bins, block), 0)

    def onehot(which):
        return jnp.where(bin_ids == ids_ref[which : which + 1, :], 1.0, 0.0).astype(jnp.bfloat16)

    first = jnp.dot(adv[...], onehot(0), preferred_element_type=jnp.float32)
    second = jnp.dot(adv[...], onehot(1), preferred_element_type=jnp.float32)
    products = (coef_ref[...] * first * second).astype(jnp.bfloat16)
    total[...] += lax.dot_general(
        products, onehot(2), (((1,), (1,)), ((), ())), preferred_element_type=jnp.float32
    )

    @pl.when(step == pl.num_programs(0) - 1)
    def _():
        out_ref[...] = (adv[...].astype(jnp.float32) + DT_SOURCE * total[...]).astype(jnp.bfloat16)


def wave_step(win, edges, mask, kernel_all, speeds, surface, wet, pair_bins, pair_coef, columns):
    bins, wide = win.shape
    cells = wide - 2 * columns
    pairs = pair_bins.shape[1]
    block = 512 if pairs % 512 == 0 else pairs
    chunk = 128 if bins % 128 == 0 else bins
    whole = lambda shape: pl.BlockSpec(shape, lambda i: (0, 0))
    return pl.pallas_call(
        functools.partial(wave_kernel, columns, chunk),
        grid=(pairs // block,),
        out_shape=jax.ShapeDtypeStruct((cells, bins), jnp.bfloat16),
        in_specs=[
            whole(win.shape),
            whole(edges.shape),
            whole(mask.shape),
            whole(kernel_all.shape),
            whole(speeds.shape),
            whole(surface.shape),
            whole(wet.shape),
            pl.BlockSpec((3, block), lambda i: (0, i)),
            pl.BlockSpec((1, block), lambda i: (0, i)),
        ],
        out_specs=whole((cells, bins)),
        scratch_shapes=[
            pltpu.VMEM((wide, bins), jnp.bfloat16),
            pltpu.VMEM((2, wide, chunk), jnp.float32),
            pltpu.VMEM((cells, chunk), jnp.float32),
            pltpu.VMEM((cells, bins), jnp.bfloat16),
            pltpu.VMEM((cells, bins), jnp.float32),
        ],
        compiler_params=pltpu.CompilerParams(vmem_limit_bytes=48 * 1024 * 1024),
        cost_estimate=pl.CostEstimate(
            flops=6 * pairs * bins * cells, bytes_accessed=4 * bins * wide, transcendentals=0
        ),
        name="wave_step",
    )(win, edges, mask, kernel_all, speeds, surface, wet, pair_bins, pair_coef[None, :])


def per_device(
    spectrum,
    group_speed,
    stokes_kernel,
    pair_bins,
    pair_coef,
    currents,
    col_map,
    wave_wet,
    ocean_wet,
):
    local_bins, tile_rows, columns = spectrum.shape
    space_count = lax.axis_size("space")
    bins_count = lax.axis_size("bins")
    groups = space_count * bins_count
    group_cols = columns // groups
    levels = stokes_kernel.shape[1] // 2
    block_rows = tile_rows // bins_count
    width = block_rows * columns
    slot_col = (
        col_map[:, None] * group_cols + jnp.arange(group_cols, dtype=jnp.int32)[None, :]
    ).reshape(-1)

    window_rows = block_rows + 2
    surface = surface_windows(currents, ocean_wet, levels, block_rows)[:, None, :]

    rows = spectrum.reshape(local_bins, bins_count, width)
    zeros = jnp.zeros((local_bins, 1, columns), spectrum.dtype)
    before = jnp.concatenate([zeros, rows[:, :-1, width - columns :]], axis=1)
    after = jnp.concatenate([rows[:, 1:, :columns], zeros], axis=1)
    windows = jnp.transpose(jnp.concatenate([before, after, rows], axis=2), (1, 0, 2))
    zero = zeros[:, 0]
    edges = jnp.stack(
        [
            jnp.concatenate([spectrum[:, -1, :], zero], axis=1),
            jnp.concatenate([zero, spectrum[:, 0, :]], axis=1),
        ]
    )
    speeds = jnp.pad(group_speed, ((0, -2 % 8), (0, -local_bins % 128)))
    win, kernel_all, speeds, edges, surface = exchange(
        windows, stokes_kernel, speeds, edges, surface, space_count, bins_count
    )
    speeds = jnp.transpose(speeds[:, :2, :local_bins], (1, 0, 2)).reshape(2, -1)
    space, part = lax.axis_index("space"), lax.axis_index("bins")
    from_below = (part == 0) & (space > 0)
    from_above = (part == bins_count - 1) & (space < space_count - 1)
    is_below = jnp.arange(2 * columns, dtype=jnp.int32) < columns
    take_edge = jnp.where(is_below, from_below, from_above)
    take_edge = take_edge.astype(jnp.float32)[None, :]
    drift_main = lax.dot_general(
        win[:, 2 * columns :],
        kernel_all,
        (((0,), (0,)), ((), ())),
        preferred_element_type=jnp.float32,
    )
    mine = surface[:, 0, : 8 * window_rows].reshape(groups, window_rows, 8)
    mine = mine[:, :, : 3 * group_cols].reshape(groups, window_rows, 3, group_cols)
    mine = jnp.transpose(mine, (0, 3, 2, 1)).reshape(groups * group_cols, 3, window_rows)
    here = slot_col[:, None] == jnp.arange(columns, dtype=jnp.int32)[None, :]
    mine = jnp.sum(jnp.where(here[:, None, None, :], mine[:, :, :, None], 0.0), axis=0)
    mine = mine.reshape(3, window_rows * columns)
    wet_rows = wave_wet.astype(jnp.float32).reshape(bins_count, block_rows, columns)
    is_mine = jnp.arange(bins_count, dtype=jnp.int32) == part
    wet_rows = jnp.sum(jnp.where(is_mine[:, None, None], wet_rows, 0.0), axis=0).reshape(1, width)

    inner = drift_main.reshape(block_rows, columns, 2 * levels)
    routed = jnp.einsum(
        "jc,xcl->jxl",
        here.astype(jnp.bfloat16),
        inner.astype(jnp.bfloat16),
        preferred_element_type=jnp.float32,
    ).astype(jnp.bfloat16)
    drift = lax.all_to_all(
        routed, ("space", "bins"), split_axis=0, concat_axis=0, tiled=True
    )
    new_currents = ocean_step(currents, drift, ocean_wet, levels)

    updated = wave_step(
        win, edges, take_edge, kernel_all, speeds, mine, wet_rows, pair_bins, pair_coef, columns
    )
    new_spectrum = jnp.transpose(
        updated.reshape(block_rows, columns, bins_count * local_bins), (2, 0, 1)
    )
    return (new_spectrum, new_currents)


def solution(mesh):
    placed = (
        P("bins", "space", None),
        P(None, "bins"),
        P("bins", None),
        P(),
        P(),
        P(("space", "bins"), None, None),
        P(),
        P("space", None),
        P(("space", "bins"), None),
    )
    return jax.shard_map(
        per_device,
        mesh=mesh,
        in_specs=placed,
        out_specs=(P(None, ("space", "bins"), None), P(("space", "bins"), None, None)),
        check_vma=False,
    )
```
